256 devices in a mesh: row: 32 (over z, x), col: 8 (over y, core).
Axes of the slice: x: 4, y: 4, z: 8, core: 2. Of those that a mesh axis runs over, the one named last changes fastest.
Arguments:
- rhs: bfloat16 [4, 8192, 256], P(None, 'row'), may hold values from -6 to 6
- dinv: bfloat16 [4, 8192, 256], P(None, 'row'), may hold values from -0.125 to 1.1875, as said below
- factor: bfloat16 [6, 8192, 24, 256], P(None, 'row', 'col'), may hold values from -0.046875 to 0.046875
- cols: int32 [6, 32, 24], P(None, 'row', 'col'), may hold values from 0 to 31, as said below
- live: int32 [6, 32], P(None, 'row'), may hold values from 1 to 24, as said below
Outputs:
- solved: float32 [4, 8192, 256], P(None, 'row', 'col')
The draws below stay inside these ranges and needn't reach their ends.
Inputs may be any that keep to these rules, and one draw needn't show every extreme that they name: Each 256 x 256 block of dinv is lower triangular with diagonal entries from about 0.6 to 1.1875. `cols`: the 24 slots of one tile row and level pair name distinct tile columns. Every level pair has a tile row with all 24 slots live and one with a single live slot.
All inputs are finite; a program needn't handle non-finite values.
Results may differ from the reference program's by a relative error of at most 0.003.
Values may be sent and summed in bfloat16 or wider, within the bound.
No kernel may reach another device: no remote copies, remote signals or barrier semaphores. Data moves between devices by JAX's collectives and lax.ppermute only.
A program may use at most 64 MiB of HBM per device.

```python
import math
import jax
import jax.numpy as jnp
from jax import lax

TILE = 256
LEVELS = 4
PROBES = 256
NT = 32
ROWS = 8192
NB = 24
PAIRS = 6


def draw_dinv(key, part):
    key = jax.random.fold_in(key, 11)
    key_diag, key_lower = jax.random.split(key)
    row_within = (jnp.arange(ROWS) % TILE)[None, :, None]
    col_within = jnp.arange(TILE)[None, None, :]
    lower = 0.5 * jax.random.normal(key_lower, (LEVELS, ROWS, TILE), jnp.float32)
    lower = jnp.clip(lower / math.sqrt(TILE), -0.125, 0.125)
    diagonal = jax.random.uniform(key_diag, (LEVELS, ROWS, 1), jnp.float32, 0.6, 1.2)
    diagonal = jnp.minimum(diagonal, 1.1875)
    values = jnp.where(col_within < row_within, lower, 0.0) + jnp.where(col_within == row_within, diagonal, 0.0)
    return values.astype(jnp.bfloat16)


def draw_cols(key, part):
    key = jax.random.fold_in(key, 37)
    scores = jax.random.randint(key, (PAIRS, NT, NT), 0, 2 ** 20) * NT + jnp.arange(NT, dtype=jnp.int32)[None, None, :]
    order = jnp.argsort(scores, axis=2)
    return order[:, :, :NB].astype(jnp.int32)


def draw_live(key, part):
    key = jax.random.fold_in(key, 23)
    key_base, key_top, key_step = jax.random.split(key, 3)
    counts = jax.random.randint(key_base, (PAIRS, NT), 1, NB + 1)
    top_place = jax.random.randint(key_top, (PAIRS, 1), 0, NT)
    single_place = (top_place + jax.random.randint(key_step, (PAIRS, 1), 1, NT)) % NT
    places = jnp.arange(NT)[None, :]
    counts = jnp.where(places == top_place, NB, counts)
    counts = jnp.where(places == single_place, 1, counts)
    return counts.astype(jnp.int32)


def levels(key, dims, cuts, least, high):
    factor_of, own = 1.0, jax.random.fold_in(key, 6)
    for dim, shards_of in cuts:
        draws = jnp.exp(jax.random.uniform(jax.random.fold_in(own, dim), (shards_of,), jnp.float32, least / len(cuts), high / len(cuts)))
        factor_of = factor_of * jnp.repeat(draws, dims[dim] // shards_of).reshape([-1 if axis == dim else 1 for axis in range(len(dims))])
    return factor_of


def bell_draw(stream_key, dims, scale, bound, cuts=(), kind=jnp.bfloat16):
    drawn = scale * jax.random.normal(stream_key, dims, jnp.float32)
    if cuts:
        drawn = drawn * levels(stream_key, dims, cuts, -0.22, 0.18)
    return jnp.clip(drawn, -bound, bound).astype(kind)


def setup_inputs(seed: int = 0) -> dict:
    key_of = jax.random.split(jax.random.key(seed), 6)
    rhs = bell_draw(key_of[0], (LEVELS, ROWS, PROBES), 1.0, 6.0, ((1, 32),))
    dinv = draw_dinv(jax.random.fold_in(key_of[5], 71), 0)
    factor = bell_draw(key_of[2], (PAIRS, ROWS, NB, TILE), (TILE * NB * (LEVELS - 1)) ** -0.5, 0.046875, ((1, 32), (2, 8)))
    cols = draw_cols(jax.random.fold_in(key_of[5], 71), 0)
    live = draw_live(jax.random.fold_in(key_of[5], 71), 0)
    return {"rhs": rhs, "dinv": dinv, "factor": factor, "cols": cols, "live": live}


def reference(rhs, dinv, factor, cols, live):
    results = []
    finished = []
    for target in range(LEVELS):
        updates = jnp.zeros((ROWS, PROBES), jnp.float32)
        for anchor in range(target):
            pair_slot = target * (target - 1) // 2 + anchor
            ready_tiles = finished[anchor]

            def row_update(packed):
                factor_row, column_ids, live_count = packed
                live_mask = (jnp.arange(NB) < live_count).astype(jnp.bfloat16)
                chosen = ready_tiles[column_ids.astype(jnp.int32)] * live_mask[:, None, None]
                return jnp.dot(factor_row.reshape(TILE, NB * TILE), chosen.reshape(NB * TILE, PROBES), preferred_element_type=jnp.float32)

            contrib = lax.map(row_update, (factor[pair_slot].reshape(NT, TILE, NB, TILE), cols[pair_slot], live[pair_slot]))
            updates = updates + contrib.reshape(ROWS, PROBES)
        residual = (rhs[target].astype(jnp.float32) - updates).astype(jnp.bfloat16)
        answer = jnp.einsum("tab,tbq->taq", dinv[target].reshape(NT, TILE, TILE).astype(jnp.float32), residual.reshape(NT, TILE, PROBES).astype(jnp.float32), precision=lax.Precision.HIGHEST)
        answer = answer.reshape(ROWS, PROBES)
        results.append(answer)
        finished.append(answer.astype(jnp.bfloat16).reshape(NT, TILE, PROBES))
    return jnp.stack(results)
```

```python
import functools

import jax
import jax.numpy as jnp
from jax import lax
from jax.experimental import pallas as pl
from jax.experimental.pallas import tpu as pltpu
from jax.sharding import PartitionSpec as P

NT_DIMS = (((1,), (1,)), ((), ()))


def dot_nt(a, b):
    return lax.dot_general(a, b, NT_DIMS, preferred_element_type=jnp.float32)


def probe_rows(place, rhs):
    block = 32
    probe = lax.broadcasted_iota(jnp.int32, (block, rhs.shape[1]), 1)
    mine = lax.broadcasted_iota(jnp.int32, (block, rhs.shape[1]), 0) + place * block
    return dot_nt((probe == mine).astype(jnp.bfloat16), rhs)


def level_kernel(level, copies, *refs):
    place, cols, live = refs[:3]
    rhs, dinv = refs[3:5]
    known = refs[5 : 5 + level]
    tiles = refs[5 + level : 5 + 2 * level]
    answer, spread = refs[5 + 2 * level :]
    total = probe_rows(place[0], rhs[0])
    base = level * (level - 1) // 2
    slots = cols.shape[1]
    update = jnp.zeros_like(total)
    for anchor in range(level):
        pair = base + anchor
        for slot in range(slots):
            block = known[anchor][cols[pair, slot]]
            block = jnp.where(slot < live[pair, 0], block, jnp.zeros_like(block))
            update = update + dot_nt(block, tiles[anchor][slot])
    residual = (total - update).astype(jnp.bfloat16)
    result = dot_nt(residual, dinv[0])
    answer[...] = result
    if copies:
        rounded = result.astype(jnp.bfloat16)
        for copy in range(copies):
            spread[copy] = rounded


def level_call(level, copies, place, cols, live, rhs, dinv, known, tiles):
    size = dinv.shape[2]
    smem = pl.BlockSpec(memory_space=pltpu.SMEM)
    vmem = pl.BlockSpec(memory_space=pltpu.VMEM)
    pick = pl.BlockSpec((1, size, size), lambda i: (level, 0, 0))
    count = max(copies, 1)
    whole = lambda a: pl.BlockSpec(a.shape, lambda i, n=a.ndim: (0,) * n)
    return pl.pallas_call(
        functools.partial(level_kernel, level, copies),
        grid=(1,),
        out_shape=(
            jax.ShapeDtypeStruct((32, size), jnp.float32),
            jax.ShapeDtypeStruct((count, 32, size), jnp.bfloat16),
        ),
        in_specs=[smem, smem, smem, pick, pick] + [whole(a) for a in known] + [whole(a) for a in tiles],
        out_specs=(
            pl.BlockSpec((32, size), lambda i: (0, 0)),
            pl.BlockSpec((count, 32, size), lambda i: (0, 0, 0)),
        ),
        compiler_params=pltpu.CompilerParams(vmem_limit_bytes=48 * 1024 * 1024),
        name="level%d" % level,
    )(place, cols, live, rhs, dinv, *known, *tiles)


def local(rhs, dinv, factor, cols, live):
    levels = rhs.shape[0]
    rows = lax.axis_size("row")
    place = lax.axis_index("col").astype(jnp.int32).reshape(1)
    tiles = factor.transpose(0, 2, 1, 3)
    all_cols = lax.all_gather(cols[:, 0, :], "col", axis=1, tiled=True)
    gathered = []
    for level in range(1, levels):
        base = level * (level - 1) // 2
        part = tiles[base : base + level]
        gathered.append(lax.all_gather(part, "col", axis=1, tiled=True))
    known, answers = [], []
    for level in range(levels):
        copies = rows if level + 1 < levels else 0
        use = [gathered[level - 1][a] for a in range(level)] if level else []
        answer, spread = level_call(level, copies, place, all_cols, live, rhs, dinv, known, use)
        answers.append(answer)
        if copies:
            known.append(lax.all_to_all(spread, "row", 0, 0, tiled=True))
    return jnp.stack(answers).transpose(0, 2, 1)


def solution(mesh):
    in_specs = (
        P(None, "row", None),
        P(None, "row", None),
        P(None, "row", "col", None),
        P(None, "row", "col"),
        P(None, "row"),
    )
    out_specs = P(None, "row", "col")
    return jax.shard_map(local, mesh=mesh, in_specs=in_specs, out_specs=out_specs, check_vma=False)
```

```python
import functools

import jax
import jax.numpy as jnp
from jax import lax
from jax.experimental import pallas as pl
from jax.experimental.pallas import tpu as pltpu
from jax.sharding import PartitionSpec as P

NT_DIMS = (((1,), (1,)), ((), ()))
BLOCK = 32
SMEM = pl.BlockSpec(memory_space=pltpu.SMEM)
ANY = pl.BlockSpec(memory_space=pl.ANY)
CHIPS = 4
SAME = [(2 * y, 2 * ((y + 1) % CHIPS)) for y in range(CHIPS)] + [
    (2 * y + 1, 2 * ((y - 1) % CHIPS) + 1) for y in range(CHIPS)
]
CROSS = [(2 * y + 1, 2 * ((y + 1) % CHIPS)) for y in range(CHIPS)] + [
    (2 * y, 2 * ((y - 1) % CHIPS) + 1) for y in range(CHIPS)
]
FAR = [(p, (p + 4) % 8) for p in range(8)]
SWAP = [(p, p ^ 1) for p in range(8)]


def dot_nt(a, b):
    return lax.dot_general(a, b, NT_DIMS, preferred_element_type=jnp.float32)


def probe_rows(place, rhs):
    probe = lax.broadcasted_iota(jnp.int32, (BLOCK, rhs.shape[1]), 1)
    mine = lax.broadcasted_iota(jnp.int32, (BLOCK, rhs.shape[1]), 0) + place * BLOCK
    return dot_nt((probe == mine).astype(jnp.bfloat16), rhs)


def owners(place):
    chip, core = lax.div(place, 2), lax.rem(place, 2)
    out = []
    for c in (core, 1 - core):
        near = lax.rem(chip + 3 + 2 * c, CHIPS)
        far = lax.rem(chip + 2, CHIPS)
        out += [chip * 2 + c, near * 2 + c, near * 2 + 1 - c, far * 2 + c]
    return out


def spread_out(result, spread):
    rounded = result.astype(jnp.bfloat16)
    for copy in range(spread.shape[0]):
        spread[copy] = rounded


def first_kernel(cuts, place, rhs, dinv, tiles, answer, spread, *rest):
    parts, sems = rest[: len(cuts)], rest[len(cuts)]
    copies = [
        pltpu.make_async_copy(tiles.at[pl.ds(low, high - low)], part, sems.at[n])
        for n, ((low, high), part) in enumerate(zip(cuts, parts))
    ]
    for copy in copies:
        copy.start()
    residual = probe_rows(place[0], rhs[0]).astype(jnp.bfloat16)
    result = dot_nt(residual, dinv[0])
    answer[...] = result
    spread_out(result, spread)
    for copy in copies:
        copy.wait()


def first_call(rows, cuts, place, rhs, dinv, tiles):
    size = dinv.shape[2]
    pick = pl.BlockSpec((1, size, size), lambda i: (0, 0, 0))
    return pl.pallas_call(
        functools.partial(first_kernel, cuts),
        grid=(1,),
        out_shape=(
            jax.ShapeDtypeStruct((BLOCK, size), jnp.float32),
            jax.ShapeDtypeStruct((rows, BLOCK, size), jnp.bfloat16),
        )
        + tuple(jax.ShapeDtypeStruct((high - low,) + tiles.shape[1:], tiles.dtype) for low, high in cuts),
        in_specs=[SMEM, pick, pick, ANY],
        out_specs=(
            pl.BlockSpec((BLOCK, size), lambda i: (0, 0)),
            pl.BlockSpec((rows, BLOCK, size), lambda i: (0, 0, 0)),
        )
        + (ANY,) * len(cuts),
        scratch_shapes=[pltpu.SemaphoreType.DMA((len(cuts),))],
        name="level0",
    )(place, rhs, dinv, tiles)


def sum_kernel(pairs, flavours, begin, end, place, cols_here, cols_there, live, *refs):
    refs = list(refs)
    start = refs.pop(0)
    dinv = refs.pop(0) if end else None
    known = [refs.pop(0) for _ in pairs]
    tiles = [[refs.pop(0) for _ in range(1 if whole else 8)] for whole in flavours]
    total = probe_rows(place[0], start[0]) if begin else start[...]
    owner = owners(place[0])
    slots = cols_here.shape[2]
    update = jnp.zeros_like(total)
    for n, pair in enumerate(pairs):
        for piece in range(8):
            cols = cols_here if piece < 4 else cols_there
            for slot in range(slots):
                block = known[n][cols[piece % 4, pair, slot]]
                alive = owner[piece] * slots + slot < live[pair, 0]
                block = jnp.where(alive, block, jnp.zeros_like(block))
                if flavours[n]:
                    tile = tiles[n][0][0, owner[piece] * slots + slot]
                else:
                    tile = tiles[n][piece][0, slot]
                update = update + dot_nt(block, tile)
    total = total - update
    if not end:
        refs[0][...] = total
        return
    result = dot_nt(total.astype(jnp.bfloat16), dinv[0])
    refs[0][...] = result
    if len(refs) > 1:
        spread_out(result, refs[1])


def sum_call(name, level, pairs, begin, end, rows, scalars, start, dinv, known, tiles):
    size = dinv.shape[2]
    pick = pl.BlockSpec((1, size, size), lambda i: (level, 0, 0))
    flat = pl.BlockSpec((BLOCK, size), lambda i: (0, 0))
    cube = pl.BlockSpec((32, BLOCK, size), lambda i: (0, 0, 0))
    args = list(scalars) + [start]
    specs = [SMEM] * 4 + [pick if begin else flat]
    if end:
        args.append(dinv)
        specs.append(pick)
    for array in known:
        args.append(array)
        specs.append(cube)
    flavours = tuple(len(group) == 1 for group in tiles)
    for group in tiles:
        for array, index in group:
            args.append(array)
            specs.append(pl.BlockSpec((1,) + array.shape[1:], lambda i, n=index: (n, 0, 0, 0)))
    out_shape = [jax.ShapeDtypeStruct((BLOCK, size), jnp.float32)]
    out_specs = [flat]
    if end and rows:
        out_shape.append(jax.ShapeDtypeStruct((rows, BLOCK, size), jnp.bfloat16))
        out_specs.append(pl.BlockSpec((rows, BLOCK, size), lambda i: (0, 0, 0)))
    count = len(pairs)
    return pl.pallas_call(
        functools.partial(sum_kernel, tuple(pairs), flavours, begin, end),
        grid=(1,),
        out_shape=tuple(out_shape),
        in_specs=specs,
        out_specs=tuple(out_specs),
        cost_estimate=pl.CostEstimate(
            flops=2 * 24 * count * size * size * size, bytes_accessed=count * 24 * size * size * 2, transcendentals=0
        ),
        compiler_params=pltpu.CompilerParams(vmem_limit_bytes=40 * 1024 * 1024),
        name=name,
    )(*args)


def local(rhs, dinv, factor, cols, live):
    rows = lax.axis_size("row")
    place = lax.axis_index("col").astype(jnp.int32).reshape(1)
    tiles = factor.transpose(0, 2, 1, 3)
    move = lambda array, pairs: lax.ppermute(array, "col", pairs)

    answer0, spread0, part1, part2, part3 = first_call(rows, ((0, 1), (1, 3), (3, 6)), place, rhs, dinv, tiles)

    def ring(part, forward):
        same, cross = move(part, SAME), move(part, CROSS)
        far = move(same, SAME) if forward else move(part, FAR)
        return [same, cross, far]

    got1 = ring(part1, False)
    got2 = ring(part2, True)
    own = cols[:, 0, :]
    cols_here = jnp.stack([own, move(own, SAME), move(own, CROSS), move(own, FAR)])
    cols_there = move(cols_here, SWAP)
    swapped = move(tiles, SWAP)
    gathered3 = lax.all_gather(part3, "col", axis=1, tiled=True)

    there1 = [move(a, SWAP) for a in got1]
    there2 = [move(a, SWAP) for a in got2]

    def pieces(pair, index, part, got, there):
        return [(part, index)] + [(a, index) for a in got] + [(swapped, pair)] + [(a, index) for a in there]

    scalars = (place, cols_here, cols_there, live)
    known0 = lax.all_to_all(spread0, "row", 0, 0, tiled=True)
    answer1, spread1 = sum_call(
        "level1", 1, (0,), True, True, rows, scalars, rhs, dinv, [known0], [pieces(0, 0, part1, got1, there1)]
    )
    known1 = lax.all_to_all(spread1, "row", 0, 0, tiled=True)
    (early2,) = sum_call(
        "early2", 2, (1,), True, False, 0, scalars, rhs, dinv, [known0], [pieces(1, 0, part2, got2, there2)]
    )
    answer2, spread2 = sum_call(
        "level2", 2, (2,), False, True, rows, scalars, early2, dinv, [known1], [pieces(2, 1, part2, got2, there2)]
    )
    known2 = lax.all_to_all(spread2, "row", 0, 0, tiled=True)
    (early3,) = sum_call(
        "early3", 3, (3, 4), True, False, 0, scalars, rhs, dinv, [known0, known1], [[(gathered3, 0)], [(gathered3, 1)]]
    )
    (answer3,) = sum_call(
        "level3", 3, (5,), False, True, 0, scalars, early3, dinv, [known2], [[(gathered3, 2)]]
    )
    return jnp.stack([answer0, answer1, answer2, answer3]).transpose(0, 2, 1)


def solution(mesh):
    in_specs = (
        P(None, "row", None),
        P(None, "row", None),
        P(None, "row", "col", None),
        P(None, "row", "col"),
        P(None, "row"),
    )
    out_specs = P(None, "row", "col")
    return jax.shard_map(local, mesh=mesh, in_specs=in_specs, out_specs=out_specs, check_vma=False)
```

```python
import functools

import jax
import jax.numpy as jnp
from jax import lax
from jax.experimental import pallas as pl
from jax.experimental.pallas import tpu as pltpu
from jax.sharding import PartitionSpec as P

NT_DIMS = (((1,), (1,)), ((), ()))
BLOCK = 32
SIZE = 256
SLOTS = 3
PLACES = 8
CHIPS = 4
PAIRS = 6
NT = 32
EXTRA = 16
CHUNK = SLOTS * SIZE + EXTRA
VMEM_BYTES = 56 * 1024 * 1024
SMEM = pl.BlockSpec(memory_space=pltpu.SMEM)
ANY = pl.BlockSpec(memory_space=pl.ANY)
F32, BF16 = jnp.float32, jnp.bfloat16
SAME = [(2 * y, 2 * ((y + 1) % CHIPS)) for y in range(CHIPS)] + [
    (2 * y + 1, 2 * ((y - 1) % CHIPS) + 1) for y in range(CHIPS)
]
CROSS = [(2 * y + 1, 2 * ((y + 1) % CHIPS)) for y in range(CHIPS)] + [
    (2 * y, 2 * ((y - 1) % CHIPS) + 1) for y in range(CHIPS)
]
FAR = [(p, (p + 4) % 8) for p in range(8)]
SWAP = [(p, p ^ 1) for p in range(8)]
TURN = [[(p, (p + 2 * d) % 8) for p in range(8)] for d in range(CHIPS)]


def dot_nt(a, b):
    return lax.dot_general(a, b, NT_DIMS, preferred_element_type=F32)


def block_of(shape, *lead):
    return pl.BlockSpec(shape, lambda i: tuple(lead) + (0,) * (len(shape) - len(lead)))


def probe_rows(place, rhs):
    probe = lax.broadcasted_iota(jnp.int32, (BLOCK, rhs.shape[1]), 1)
    mine = lax.broadcasted_iota(jnp.int32, (BLOCK, rhs.shape[1]), 0) + place * BLOCK
    return dot_nt((probe == mine).astype(BF16), rhs)


def owners(place):
    chip, core = lax.div(place, 2), lax.rem(place, 2)
    out = []
    for c in (core, 1 - core):
        near = lax.rem(chip + 3 + 2 * c, CHIPS)
        far = lax.rem(chip + 2, CHIPS)
        out += [chip * 2 + c, near * 2 + c, near * 2 + 1 - c, far * 2 + c]
    return out


def spread_out(result, spread):
    rounded = result.astype(BF16)
    for copy in range(spread.shape[0]):
        spread[copy] = rounded


def call(kernel, name, shapes, in_specs, out_specs, args, scratch=(), flops=0, moved=0):
    return pl.pallas_call(
        kernel,
        grid=(1,),
        out_shape=tuple(jax.ShapeDtypeStruct(s, t) for s, t in shapes),
        in_specs=in_specs,
        out_specs=tuple(out_specs),
        scratch_shapes=list(scratch),
        cost_estimate=pl.CostEstimate(flops=flops, bytes_accessed=moved, transcendentals=0),
        compiler_params=pltpu.CompilerParams(vmem_limit_bytes=VMEM_BYTES),
        name=name,
    )(*args)


def first_kernel(place, cols, rhs, dinv, tiles, answer, spread, chunk):
    residual = probe_rows(place[0], rhs[0]).astype(BF16)
    result = dot_nt(residual, dinv[0])
    answer[...] = result
    spread_out(result, spread)
    for slot in range(SLOTS):
        chunk[slot * SIZE : (slot + 1) * SIZE] = tiles[0, slot]
    lane = lax.broadcasted_iota(jnp.int32, (EXTRA, SIZE), 1)
    packed = jnp.zeros((EXTRA, SIZE), jnp.int32)
    for pair in range(PAIRS):
        for slot in range(SLOTS):
            packed = jnp.where(lane == pair * SLOTS + slot, cols[pair, slot], packed)
    chunk[SLOTS * SIZE :] = packed.astype(F32).astype(BF16)


def first_call(place, cols, rhs, dinv, tiles):
    return call(
        first_kernel,
        "level0",
        [((BLOCK, SIZE), F32), ((NT, BLOCK, SIZE), BF16), ((CHUNK, SIZE), BF16)],
        [SMEM, SMEM, block_of((1, SIZE, SIZE), 0), block_of((1, SIZE, SIZE), 0), block_of((1, SLOTS, SIZE, SIZE), 0)],
        [block_of((BLOCK, SIZE)), block_of((NT, BLOCK, SIZE)), block_of((CHUNK, SIZE))],
        (place, cols, rhs, dinv, tiles),
        moved=2**21,
    )


def decode_kernel(*refs):
    for piece in range(PLACES):
        refs[PLACES][pl.ds(piece, 1), :] = refs[piece][0:1, :].astype(F32).astype(jnp.int32)


def decode_call(chunks):
    spec = pl.BlockSpec((EXTRA, SIZE), lambda i: (SLOTS * SIZE // EXTRA, 0))
    return call(
        decode_kernel,
        "cols",
        [((PLACES, SIZE), jnp.int32)],
        [spec] * PLACES,
        [block_of((PLACES, SIZE))],
        chunks,
    )[0]


def masked(block, alive):
    return jnp.where(alive, block, jnp.zeros_like(block))


def level1_kernel(place, table, live, rhs, dinv, known, *refs):
    chunks, (answer, spread, held, sems) = refs[:PLACES], refs[PLACES:]
    copies = [pltpu.make_async_copy(chunks[n].at[pl.ds(0, SLOTS * SIZE)], held.at[n], sems.at[n]) for n in range(PLACES)]
    for copy in copies:
        copy.start()
    total = probe_rows(place[0], rhs[0])
    owner = owners(place[0])
    for piece in range(PLACES):
        copies[piece].wait()
        for slot in range(SLOTS):
            block = masked(known[table[piece, slot]], owner[piece] * SLOTS + slot < live[0, 0])
            total = total - dot_nt(block, held[piece, slot * SIZE : (slot + 1) * SIZE])
    result = dot_nt(total.astype(BF16), dinv[0])
    answer[...] = result
    spread_out(result, spread)


def level1_call(place, table, live, rhs, dinv, known, chunks):
    pick = block_of((1, SIZE, SIZE), 1)
    return call(
        level1_kernel,
        "level1",
        [((BLOCK, SIZE), F32), ((NT, BLOCK, SIZE), BF16)],
        [SMEM] * 3 + [pick, pick, block_of((NT, BLOCK, SIZE))] + [ANY] * PLACES,
        [block_of((BLOCK, SIZE)), block_of((NT, BLOCK, SIZE))],
        (place, table, live, rhs, dinv, known, *chunks),
        [pltpu.VMEM((PLACES, SLOTS * SIZE, SIZE), BF16), pltpu.SemaphoreType.DMA((PLACES,))],
        flops=2 * 24 * BLOCK * SIZE * SIZE,
        moved=24 * SIZE * SIZE * 2,
    )


def pick_kernel(pairs, place, table, known, *outs):
    owner = owners(place[0])
    chip = lax.div(place[0], 2)
    for step in range(CHIPS):
        for core in range(2):
            want = lax.rem(chip + step, CHIPS) * 2 + core
            piece = jnp.int32(0)
            for n in range(PLACES):
                piece = jnp.where(owner[n] == want, n, piece)
            for n, pair in enumerate(pairs):
                for slot in range(SLOTS):
                    outs[step][n, core * SLOTS + slot] = known[table[piece, pair * SLOTS + slot]]


def pick_call(pairs, place, table, known):
    shape = (len(pairs), 2 * SLOTS, BLOCK, SIZE)
    return call(
        functools.partial(pick_kernel, pairs),
        "pick",
        [(shape, BF16)] * CHIPS,
        [SMEM, SMEM, block_of((NT, BLOCK, SIZE))],
        [block_of(shape)] * CHIPS,
        (place, table, known),
        moved=2**21,
    )


def partial_kernel(pairs, place, live, *refs):
    got, mine, theirs, outs = refs[:CHIPS], refs[CHIPS :: 2], refs[CHIPS + 1 :: 2], refs[-CHIPS:]
    chip, core = lax.div(place[0], 2), lax.rem(place[0], 2)
    for n, pair in enumerate(pairs):
        total = jnp.zeros((CHIPS * BLOCK, SIZE), F32)
        for swapped in range(2):
            side = lax.rem(core + swapped, 2)
            for slot in range(SLOTS):
                at = side * SLOTS + slot
                block = jnp.concatenate([g[n, at] for g in got])
                block = masked(block, chip * 2 * SLOTS + at < live[pair, 0])
                total = total + dot_nt(block, (theirs if swapped else mine)[n][0, slot])
        for step in range(CHIPS):
            outs[step][n] = total[step * BLOCK : (step + 1) * BLOCK]


def partial_call(pairs, place, live, got, tiles, swapped):
    shape = (len(pairs), BLOCK, SIZE)
    args, specs = [place, live, *got], [SMEM, SMEM] + [block_of(g.shape) for g in got]
    for pair in pairs:
        args += [tiles, swapped]
        specs += [block_of((1, SLOTS, SIZE, SIZE), pair)] * 2
    return call(
        functools.partial(partial_kernel, pairs),
        "partial",
        [(shape, F32)] * CHIPS,
        specs,
        [block_of(shape)] * CHIPS,
        args,
        flops=2 * 6 * SIZE**3,
        moved=2**21,
    )


def whole_kernel(index, pair, begin, part, finish, place, table, live, start, known, tiles, *refs):
    refs = list(refs)
    back = [refs.pop(0) for _ in range(CHIPS)] if part is not None else []
    dinv = refs.pop(0) if finish else None
    earlier = [refs.pop(0) for _ in range(3)] if finish == "last" else []
    held, sems = refs[-2:]
    owner = owners(place[0])
    copies = [
        pltpu.make_async_copy(tiles.at[index, pl.ds(owner[n] * SLOTS, SLOTS)], held.at[n], sems.at[n])
        for n in range(PLACES)
    ]
    for copy in copies:
        copy.start()
    total = probe_rows(place[0], start[0]) if begin else start[...]
    for sums in back:
        total = total - sums[part]
    for piece in range(PLACES):
        copies[piece].wait()
        for slot in range(SLOTS):
            block = masked(known[table[piece, pair * SLOTS + slot]], owner[piece] * SLOTS + slot < live[pair, 0])
            total = total - dot_nt(block, held[piece, slot])
    if not finish:
        refs[0][...] = total
        return
    result = dot_nt(total.astype(BF16), dinv[0])
    if finish == "last":
        for n in range(3):
            refs[0][n] = earlier[n][...]
        refs[0][3] = result
        return
    refs[0][...] = result
    spread_out(result, refs[1])


def whole_call(name, level, index, pair, begin, finish, place, table, live, start, known, tiles, part, back, dinv, earlier):
    flat, pick = block_of((BLOCK, SIZE)), block_of((1, SIZE, SIZE), level)
    args = [place, table, live, start, known, tiles]
    specs = [SMEM] * 3 + [pick if begin else flat, block_of((NT, BLOCK, SIZE)), ANY]
    if part is not None:
        args += back
        specs += [block_of(b.shape) for b in back]
    if finish:
        args.append(dinv)
        specs.append(pick)
    if finish == "last":
        args += earlier
        specs += [flat] * 3
        shapes, outs = [((4, BLOCK, SIZE), F32)], [block_of((4, BLOCK, SIZE))]
    else:
        shapes, outs = [((BLOCK, SIZE), F32)], [flat]
        if finish:
            shapes.append(((NT, BLOCK, SIZE), BF16))
            outs.append(block_of((NT, BLOCK, SIZE)))
    return call(
        functools.partial(whole_kernel, index, pair, begin, part, finish),
        name,
        shapes,
        specs,
        outs,
        args,
        [pltpu.VMEM((PLACES, SLOTS, SIZE, SIZE), BF16), pltpu.SemaphoreType.DMA((PLACES,))],
        flops=2 * 24 * BLOCK * SIZE * SIZE,
        moved=24 * SIZE * SIZE * 2,
    )


def local(rhs, dinv, factor, cols, live):
    place = lax.axis_index("col").astype(jnp.int32).reshape(1)
    tiles = factor.transpose(0, 2, 1, 3)
    move = lambda array, pairs: lax.ppermute(array, "col", pairs)
    over_row = lambda array: lax.all_to_all(array, "row", 0, 0, tiled=True)

    answer0, spread0, chunk = first_call(place, cols[:, 0, :], rhs, dinv, tiles)
    here = [chunk, move(chunk, SAME), move(chunk, CROSS), move(chunk, FAR)]
    chunks = here + [move(a, SWAP) for a in here]
    later, chunk = lax.optimization_barrier((tiles, chunk))
    gathered2 = lax.all_gather(later[2:3], "col", axis=1, tiled=True)
    gathered45 = lax.all_gather(later[4:6], "col", axis=1, tiled=True)
    swapped = move(tiles, SWAP)

    known0 = over_row(spread0)
    table = decode_call(chunks)
    answer1, spread1 = level1_call(place, table, live, rhs, dinv, known0, chunks)
    known1 = over_row(spread1)

    known0, spread1 = lax.optimization_barrier((known0, spread1))
    sent = pick_call((1, 3), place, table, known0)
    got = [sent[0]] + [move(sent[d], TURN[d]) for d in range(1, CHIPS)]
    sums = partial_call((1, 3), place, live, got, tiles, swapped)
    back = [sums[0]] + [move(sums[d], TURN[CHIPS - d]) for d in range(1, CHIPS)]

    answer2, spread2 = whole_call(
        "level2", 2, 0, 2, True, "more", place, table, live, rhs, known1, gathered2, 0, back, dinv, None
    )
    known2 = over_row(spread2)
    (early3,) = whole_call(
        "early3", 3, 0, 4, True, "", place, table, live, rhs, known1, gathered45, 1, back, None, None
    )
    (solved,) = whole_call(
        "level3", 3, 1, 5, False, "last", place, table, live, early3, known2, gathered45, None, None, dinv,
        [answer0, answer1, answer2],
    )
    return solved.transpose(0, 2, 1)


def solution(mesh):
    in_specs = (
        P(None, "row", None),
        P(None, "row", None),
        P(None, "row", "col", None),
        P(None, "row", "col"),
        P(None, "row"),
    )
    out_specs = P(None, "row", "col")
    return jax.shard_map(local, mesh=mesh, in_specs=in_specs, out_specs=out_specs, check_vma=False)
```

```python
import functools

import jax
import jax.numpy as jnp
from jax import lax
from jax.experimental import pallas as pl
from jax.experimental.pallas import tpu as pltpu
from jax.sharding import PartitionSpec as P

NT_DIMS = (((1,), (1,)), ((), ()))
BLOCK = 32
SIZE = 256
SLOTS = 3
PLACES = 8
CHIPS = 4
PAIRS = 6
NT = 32
EXTRA = 16
CHUNK = SLOTS * SIZE + EXTRA
VMEM_BYTES = 56 * 1024 * 1024
SMEM = pl.BlockSpec(memory_space=pltpu.SMEM)
ANY = pl.BlockSpec(memory_space=pl.ANY)
F32, BF16 = jnp.float32, jnp.bfloat16
SWAP = [(p, p ^ 1) for p in range(PLACES)]
TURN = [[(p, (p + 2 * d) % PLACES) for p in range(PLACES)] for d in range(CHIPS)]


def dot_nt(a, b):
    return lax.dot_general(a, b, NT_DIMS, preferred_element_type=F32)


def block_of(shape, *lead):
    return pl.BlockSpec(shape, lambda i: tuple(lead) + (0,) * (len(shape) - len(lead)))


def probe_rows(place, rhs):
    probe = lax.broadcasted_iota(jnp.int32, (BLOCK, rhs.shape[1]), 1)
    mine = lax.broadcasted_iota(jnp.int32, (BLOCK, rhs.shape[1]), 0) + place * BLOCK
    return dot_nt((probe == mine).astype(BF16), rhs)


def spread_out(result, spread):
    rounded = result.astype(BF16)
    for copy in range(spread.shape[0]):
        spread[copy] = rounded


def call(kernel, name, shapes, in_specs, out_specs, args, scratch=(), flops=0, moved=0):
    return pl.pallas_call(
        kernel,
        grid=(1,),
        out_shape=tuple(jax.ShapeDtypeStruct(s, t) for s, t in shapes),
        in_specs=in_specs,
        out_specs=tuple(out_specs),
        scratch_shapes=list(scratch),
        cost_estimate=pl.CostEstimate(flops=flops, bytes_accessed=moved, transcendentals=0),
        compiler_params=pltpu.CompilerParams(vmem_limit_bytes=VMEM_BYTES),
        name=name,
    )(*args)


def first_kernel(place, cols, rhs, dinv, tiles, answer, spread, chunk):
    residual = probe_rows(place[0], rhs[0]).astype(BF16)
    result = dot_nt(residual, dinv[0])
    answer[...] = result
    spread_out(result, spread)
    for slot in range(SLOTS):
        chunk[slot * SIZE : (slot + 1) * SIZE] = tiles[0, slot]
    lane = lax.broadcasted_iota(jnp.int32, (EXTRA, SIZE), 1)
    packed = jnp.zeros((EXTRA, SIZE), jnp.int32)
    for pair in range(PAIRS):
        for slot in range(SLOTS):
            packed = jnp.where(lane == pair * SLOTS + slot, cols[slot, 0, pair], packed)
    chunk[SLOTS * SIZE :] = packed.astype(F32).astype(BF16)


def first_call(place, cols, rhs, dinv, tiles):
    return call(
        first_kernel,
        "level0",
        [((BLOCK, SIZE), F32), ((NT, BLOCK, SIZE), BF16), ((CHUNK, SIZE), BF16)],
        [SMEM, SMEM, block_of((1, SIZE, SIZE), 0), block_of((1, SIZE, SIZE), 0), block_of((1, SLOTS, SIZE, SIZE), 0)],
        [block_of((BLOCK, SIZE)), block_of((NT, BLOCK, SIZE)), block_of((CHUNK, SIZE))],
        (place, cols, rhs, dinv, tiles),
        moved=2**21,
    )


def decode_kernel(gathered, out):
    for place in range(PLACES):
        out[pl.ds(place, 1), :] = gathered[place, 0:1, :].astype(F32).astype(jnp.int32)


def decode_call(gathered):
    return call(
        decode_kernel,
        "cols",
        [((PLACES, SIZE), jnp.int32)],
        [pl.BlockSpec((PLACES, EXTRA, SIZE), lambda i: (0, SLOTS * SIZE // EXTRA, 0))],
        [block_of((PLACES, SIZE))],
        (gathered,),
    )[0]


def masked(block, alive):
    return jnp.where(alive, block, jnp.zeros_like(block))


def pick_kernel(pairs, place, table, known, *outs):
    chip = lax.div(place[0], 2)
    for step in range(CHIPS):
        for core in range(2):
            want = lax.rem(chip + step, CHIPS) * 2 + core
            for n, pair in enumerate(pairs):
                for slot in range(SLOTS):
                    outs[step][n, core * SLOTS + slot] = known[table[want, pair * SLOTS + slot]]


def pick_call(name, pairs, place, table, known):
    shape = (len(pairs), 2 * SLOTS, BLOCK, SIZE)
    return call(
        functools.partial(pick_kernel, pairs),
        name,
        [(shape, BF16)] * CHIPS,
        [SMEM, SMEM, block_of((NT, BLOCK, SIZE))],
        [block_of(shape)] * CHIPS,
        (place, table, known),
        moved=2**21,
    )


def partial_kernel(pairs, kept, place, live, *refs):
    refs = list(refs)
    got = [refs.pop(0) for _ in range(CHIPS)]
    before = [refs.pop(0) for _ in range(CHIPS)] if kept else []
    tiles = [(refs.pop(0), refs.pop(0)) for _ in pairs]
    chip, core = lax.div(place[0], 2), lax.rem(place[0], 2)
    for n, pair in enumerate(pairs):
        total = jnp.zeros((CHIPS * BLOCK, SIZE), F32)
        for swapped in range(2):
            side = lax.rem(core + swapped, 2)
            for slot in range(SLOTS):
                at = side * SLOTS + slot
                block = jnp.concatenate([g[n, at] for g in got])
                block = masked(block, chip * 2 * SLOTS + at < live[0, pair])
                total = total + dot_nt(block, tiles[n][swapped][0, slot])
        for step in range(CHIPS):
            sums = total[step * BLOCK : (step + 1) * BLOCK]
            refs[n * CHIPS + step][...] = sums + before[step][...] if kept else sums


def partial_call(name, pairs, place, live, got, kept, tiles, swapped):
    shape = (BLOCK, SIZE)
    args = [place, live, *got, *kept]
    specs = [SMEM, SMEM] + [block_of(g.shape) for g in args[2:]]
    for pair in pairs:
        args += [tiles, swapped]
        specs += [block_of((1, SLOTS, SIZE, SIZE), pair)] * 2
    return call(
        functools.partial(partial_kernel, pairs, bool(kept)),
        name,
        [(shape, F32)] * (CHIPS * len(pairs)),
        specs,
        [block_of(shape)] * (CHIPS * len(pairs)),
        args,
        flops=2 * 6 * SIZE**3,
        moved=2**21,
    )


def level_kernel(pair, returned, earlier, place, table, live, rhs, dinv, known, tiles, *refs):
    refs = list(refs)
    back = [refs.pop(0) for _ in range(returned)]
    before = [refs.pop(0) for _ in range(earlier)]
    held, sems = refs[-2:]
    copies = []
    for n in range(CHIPS):
        two = pl.ds(2 * n, 2)
        source = tiles.at[two, pl.ds(0, SLOTS * SIZE)]
        copies.append(pltpu.make_async_copy(source, held.at[two], sems.at[n]))
    for copy in copies:
        copy.start()
    total = probe_rows(place[0], rhs[0])
    for sums in back:
        total = total - sums[...]
    for owner in range(PLACES):
        if owner % 2 == 0:
            copies[owner // 2].wait()
        for slot in range(SLOTS):
            block = masked(known[table[owner, pair * SLOTS + slot]], owner * SLOTS + slot < live[0, pair])
            total = total - dot_nt(block, held[owner, slot * SIZE : (slot + 1) * SIZE])
    result = dot_nt(total.astype(BF16), dinv[0])
    if earlier:
        for n in range(earlier):
            refs[0][n] = before[n][...]
        refs[0][earlier] = result
        return
    refs[0][...] = result
    spread_out(result, refs[1])


def level_call(level, pair, place, table, live, rhs, dinv, known, tiles, back, earlier):
    flat, pick = block_of((BLOCK, SIZE)), block_of((1, SIZE, SIZE), level)
    if earlier:
        shapes, outs = [((level + 1, BLOCK, SIZE), F32)], [block_of((level + 1, BLOCK, SIZE))]
    else:
        shapes = [((BLOCK, SIZE), F32), ((NT, BLOCK, SIZE), BF16)]
        outs = [flat, block_of((NT, BLOCK, SIZE))]
    return call(
        functools.partial(level_kernel, pair, len(back), len(earlier)),
        "level%d" % level,
        shapes,
        [SMEM] * 3 + [pick, pick, block_of((NT, BLOCK, SIZE)), ANY] + [flat] * (len(back) + len(earlier)),
        outs,
        (place, table, live, rhs, dinv, known, tiles, *back, *earlier),
        [pltpu.VMEM((PLACES, SLOTS * SIZE, SIZE), BF16), pltpu.SemaphoreType.DMA((CHIPS,))],
        flops=2 * 24 * BLOCK * SIZE * SIZE,
        moved=24 * SIZE * SIZE * 2,
    )


def local(rhs, dinv, factor, cols, live):
    place = lax.axis_index("col").astype(jnp.int32).reshape(1)
    tiles = factor.transpose(0, 2, 1, 3)
    move = lambda array, pairs: lax.ppermute(array, "col", pairs)
    over_row = lambda array: lax.all_to_all(array, "row", 0, 0, tiled=True)

    gather = lambda array: lax.all_gather(array, "col", axis=0, tiled=False)
    piece = lambda array, pair: array[pair].reshape(SLOTS * SIZE, SIZE)
    live = live.transpose(1, 0)

    answer0, spread0, chunk = first_call(place, cols.transpose(2, 1, 0), rhs, dinv, tiles)
    gathered0 = gather(chunk)
    later, spread0 = lax.optimization_barrier((tiles, spread0))
    gathered2 = gather(piece(later, 2))
    gathered5 = gather(piece(later, 5))
    swapped = move(tiles, SWAP)

    def send(picked):
        return [picked[0]] + [move(picked[d], TURN[d]) for d in range(1, CHIPS)]

    def give_back(sums):
        return [sums[0]] + [move(sums[d], TURN[CHIPS - d]) for d in range(1, CHIPS)]

    known0 = over_row(spread0)
    table = decode_call(gathered0)
    answer1, spread1 = level_call(1, 0, place, table, live, rhs, dinv, known0, gathered0, [], [])
    known1 = over_row(spread1)

    known0, spread1 = lax.optimization_barrier((known0, spread1))
    got = send(pick_call("pick13", (1, 3), place, table, known0))
    sums = partial_call("partial13", (1, 3), place, live, got, [], tiles, swapped)
    sums2, sums3 = sums[:CHIPS], sums[CHIPS:]
    answer2, spread2 = level_call(2, 2, place, table, live, rhs, dinv, known1, gathered2, give_back(sums2), [])
    known2 = over_row(spread2)

    known1, spread2 = lax.optimization_barrier((known1, spread2))
    got = send(pick_call("pick4", (4,), place, table, known1))
    sums3 = partial_call("partial4", (4,), place, live, got, sums3, tiles, swapped)
    (solved,) = level_call(
        3, 5, place, table, live, rhs, dinv, known2, gathered5, give_back(sums3), [answer0, answer1, answer2]
    )
    return solved.transpose(0, 2, 1)


def solution(mesh):
    in_specs = (
        P(None, "row", None),
        P(None, "row", None),
        P(None, "row", "col", None),
        P(None, "row", "col"),
        P(None, "row"),
    )
    out_specs = P(None, "row", "col")
    return jax.shard_map(local, mesh=mesh, in_specs=in_specs, out_specs=out_specs, check_vma=False)
```

```python
import functools

import jax
import jax.numpy as jnp
from jax import lax
from jax.experimental import pallas as pl
from jax.experimental.pallas import tpu as pltpu
from jax.sharding import PartitionSpec as P

NT_DIMS = (((1,), (1,)), ((), ()))
BLOCK = 32
SIZE = 256
SLOTS = 3
PLACES = 8
CHIPS = 4
NT = 32
VMEM_BYTES = 56 * 1024 * 1024
SMEM = pl.BlockSpec(memory_space=pltpu.SMEM)
ANY = pl.BlockSpec(memory_space=pl.ANY)
F32, BF16 = jnp.float32, jnp.bfloat16
SWAP = [(p, p ^ 1) for p in range(PLACES)]
TURN = [[(p, (p + 2 * d) % PLACES) for p in range(PLACES)] for d in range(CHIPS)]


def dot_nt(a, b):
    return lax.dot_general(a, b, NT_DIMS, preferred_element_type=F32)


def block_of(shape, *lead):
    return pl.BlockSpec(shape, lambda i: tuple(lead) + (0,) * (len(shape) - len(lead)))


def probe_rows(place, rhs):
    probe = lax.broadcasted_iota(jnp.int32, (BLOCK, rhs.shape[1]), 1)
    mine = lax.broadcasted_iota(jnp.int32, (BLOCK, rhs.shape[1]), 0) + place * BLOCK
    return dot_nt((probe == mine).astype(BF16), rhs)


def spread_out(result, spread):
    rounded = result.astype(BF16)
    for copy in range(spread.shape[0]):
        spread[copy] = rounded


def call(kernel, name, shapes, in_specs, out_specs, args, scratch=(), flops=0, moved=0):
    return pl.pallas_call(
        kernel,
        grid=(1,),
        out_shape=tuple(jax.ShapeDtypeStruct(s, t) for s, t in shapes),
        in_specs=in_specs,
        out_specs=tuple(out_specs),
        scratch_shapes=list(scratch),
        cost_estimate=pl.CostEstimate(flops=flops, bytes_accessed=moved, transcendentals=0),
        compiler_params=pltpu.CompilerParams(vmem_limit_bytes=VMEM_BYTES),
        name=name,
    )(*args)


def first_kernel(place, rhs, dinv, answer, spread):
    residual = probe_rows(place[0], rhs[0]).astype(BF16)
    result = dot_nt(residual, dinv[0])
    answer[...] = result
    spread_out(result, spread)


def first_call(place, rhs, dinv):
    return call(
        first_kernel,
        "level0",
        [((BLOCK, SIZE), F32), ((NT, BLOCK, SIZE), BF16)],
        [SMEM, block_of((1, SIZE, SIZE), 0), block_of((1, SIZE, SIZE), 0)],
        [block_of((BLOCK, SIZE)), block_of((NT, BLOCK, SIZE))],
        (place, rhs, dinv),
        moved=2**22,
    )


def masked(block, alive):
    return jnp.where(alive, block, jnp.zeros_like(block))


def pick_kernel(pairs, place, here, there, known, *outs):
    mine = lax.rem(place[0], 2)
    for step in range(CHIPS):
        turn = (CHIPS - step) % CHIPS
        for core in range(2):
            for n, pair in enumerate(pairs):
                for slot in range(SLOTS):
                    at = jnp.where(mine == core, here[turn, slot, pair], there[turn, slot, pair])
                    outs[step][n, core * SLOTS + slot] = known[at]


def pick_call(name, pairs, place, here, there, known):
    shape = (len(pairs), 2 * SLOTS, BLOCK, SIZE)
    return call(
        functools.partial(pick_kernel, pairs),
        name,
        [(shape, BF16)] * CHIPS,
        [SMEM, SMEM, SMEM, block_of((NT, BLOCK, SIZE))],
        [block_of(shape)] * CHIPS,
        (place, here, there, known),
        moved=2**21,
    )


def partial_kernel(pairs, kept, place, live, *refs):
    refs = list(refs)
    got = [refs.pop(0) for _ in range(CHIPS)]
    before = [refs.pop(0) for _ in range(CHIPS)] if kept else []
    tiles = [(refs.pop(0), refs.pop(0)) for _ in pairs]
    chip, core = lax.div(place[0], 2), lax.rem(place[0], 2)
    for n, pair in enumerate(pairs):
        total = jnp.zeros((CHIPS * BLOCK, SIZE), F32)
        for swapped in range(2):
            side = lax.rem(core + swapped, 2)
            for slot in range(SLOTS):
                at = side * SLOTS + slot
                block = jnp.concatenate([g[n, at] for g in got])
                block = masked(block, chip * 2 * SLOTS + at < live[0, pair])
                total = total + dot_nt(block, tiles[n][swapped][0, slot])
        for step in range(CHIPS):
            sums = total[step * BLOCK : (step + 1) * BLOCK]
            refs[n * CHIPS + step][...] = sums + before[step][...] if kept else sums


def partial_call(name, pairs, place, live, got, kept, tiles, swapped):
    shape = (BLOCK, SIZE)
    args = [place, live, *got, *kept]
    specs = [SMEM, SMEM] + [block_of(g.shape) for g in args[2:]]
    for pair in pairs:
        args += [tiles, swapped]
        specs += [block_of((1, SLOTS, SIZE, SIZE), pair)] * 2
    return call(
        functools.partial(partial_kernel, pairs, bool(kept)),
        name,
        [(shape, F32)] * (CHIPS * len(pairs)),
        specs,
        [block_of(shape)] * (CHIPS * len(pairs)),
        args,
        flops=2 * 6 * SIZE**3,
        moved=2**21,
    )


def level_kernel(pair, returned, earlier, place, here, there, live, rhs, dinv, known, tiles, *refs):
    refs = list(refs)
    back = [refs.pop(0) for _ in range(returned)]
    before = [refs.pop(0) for _ in range(earlier)]
    held, sems = refs[-2:]
    chip, core = lax.div(place[0], 2), lax.rem(place[0], 2)
    chips = [lax.rem(chip + CHIPS - d, CHIPS) for d in range(CHIPS)]
    copies = [
        pltpu.make_async_copy(tiles.at[pl.ds(2 * chips[d], 2)], held.at[pl.ds(2 * d, 2)], sems.at[d]) for d in range(CHIPS)
    ]
    for copy in copies:
        copy.start()
    total = probe_rows(place[0], rhs[0])
    for sums in back:
        total = total - sums[...]
    for d in range(CHIPS):
        copies[d].wait()
        for cols, side in ((here, core), (there, 1 - core)):
            first = (2 * chips[d] + side) * SLOTS
            for slot in range(SLOTS):
                block = masked(known[cols[d, slot, pair]], first + slot < live[0, pair])
                total = total - dot_nt(block, held[2 * d + side, slot * SIZE : (slot + 1) * SIZE])
    result = dot_nt(total.astype(BF16), dinv[0])
    if earlier:
        for n in range(earlier):
            refs[0][n] = before[n][...]
        refs[0][earlier] = result
        return
    refs[0][...] = result
    spread_out(result, refs[1])


def level_call(level, pair, place, here, there, live, rhs, dinv, known, tiles, back, earlier):
    flat, pick = block_of((BLOCK, SIZE)), block_of((1, SIZE, SIZE), level)
    if earlier:
        shapes, outs = [((level + 1, BLOCK, SIZE), F32)], [block_of((level + 1, BLOCK, SIZE))]
    else:
        shapes = [((BLOCK, SIZE), F32), ((NT, BLOCK, SIZE), BF16)]
        outs = [flat, block_of((NT, BLOCK, SIZE))]
    return call(
        functools.partial(level_kernel, pair, len(back), len(earlier)),
        "level%d" % level,
        shapes,
        [SMEM] * 4 + [pick, pick, block_of((NT, BLOCK, SIZE)), ANY] + [flat] * (len(back) + len(earlier)),
        outs,
        (place, here, there, live, rhs, dinv, known, tiles, *back, *earlier),
        [pltpu.VMEM((PLACES, SLOTS * SIZE, SIZE), BF16), pltpu.SemaphoreType.DMA((CHIPS,))],
        flops=2 * 24 * BLOCK * SIZE * SIZE,
        moved=24 * SIZE * SIZE * 2,
    )


def local(rhs, dinv, factor, cols, live):
    place = lax.axis_index("col").astype(jnp.int32).reshape(1)
    tiles = factor.transpose(0, 2, 1, 3)
    move = lambda array, pairs: lax.ppermute(array, "col", pairs)
    over_row = lambda array: lax.all_to_all(array, "row", 0, 0, tiled=True)

    gather = lambda array: lax.all_gather(array, "col", axis=0, tiled=False)
    piece = lambda array, pair: array[pair].reshape(SLOTS * SIZE, SIZE)
    live = live.transpose(1, 0)

    own = cols.transpose(2, 1, 0).reshape(SLOTS, -1)
    here = jnp.stack([own] + [move(own, TURN[d]) for d in range(1, CHIPS)])
    there = move(here, SWAP)
    answer0, spread0 = first_call(place, rhs, dinv)
    gathered0 = gather(piece(tiles, 0))
    later, spread0 = lax.optimization_barrier((tiles, spread0))
    gathered2 = gather(piece(later, 2))
    gathered5 = gather(piece(later, 5))
    swapped = move(later, SWAP)

    def send(picked):
        return [picked[0]] + [move(picked[d], TURN[d]) for d in range(1, CHIPS)]

    def give_back(sums):
        return [sums[0]] + [move(sums[d], TURN[CHIPS - d]) for d in range(1, CHIPS)]

    known0 = over_row(spread0)
    picked = pick_call("pick13", (1, 3), place, here, there, known0)
    known0, *picked = lax.optimization_barrier((known0, *picked))
    got = send(picked)
    answer1, spread1 = level_call(1, 0, place, here, there, live, rhs, dinv, known0, gathered0, [], [])
    spread1, *got = lax.optimization_barrier((spread1, *got))
    known1 = over_row(spread1)

    sums = partial_call("partial13", (1, 3), place, live, got, [], tiles, swapped)
    sums2, sums3 = sums[:CHIPS], sums[CHIPS:]
    back2 = give_back(sums2)
    known1, *back2 = lax.optimization_barrier((known1, *back2))
    picked = pick_call("pick4", (4,), place, here, there, known1)
    known1, *picked = lax.optimization_barrier((known1, *picked))
    got = send(picked)
    answer2, spread2 = level_call(2, 2, place, here, there, live, rhs, dinv, known1, gathered2, back2, [])
    spread2, *got = lax.optimization_barrier((spread2, *got))
    known2 = over_row(spread2)

    sums3 = partial_call("partial4", (4,), place, live, got, sums3, tiles, swapped)
    (solved,) = level_call(
        3, 5, place, here, there, live, rhs, dinv, known2, gathered5, give_back(sums3), [answer0, answer1, answer2]
    )
    return solved.transpose(0, 2, 1)


def solution(mesh):
    in_specs = (
        P(None, "row", None),
        P(None, "row", None),
        P(None, "row", "col", None),
        P(None, "row", "col"),
        P(None, "row"),
    )
    out_specs = P(None, "row", "col")
    return jax.shard_map(local, mesh=mesh, in_specs=in_specs, out_specs=out_specs, check_vma=False)
```

```python
import functools

import jax
import jax.numpy as jnp
from jax import lax
from jax.experimental import pallas as pl
from jax.experimental.pallas import tpu as pltpu
from jax.sharding import PartitionSpec as P

NT_DIMS = (((1,), (1,)), ((), ()))
BLOCK = 32
SIZE = 256
SLOTS = 3
PLACES = 8
CHIPS = 4
NT = 32
VMEM_BYTES = 56 * 1024 * 1024
SMEM = pl.BlockSpec(memory_space=pltpu.SMEM)
ANY = pl.BlockSpec(memory_space=pl.ANY)
F32, BF16 = jnp.float32, jnp.bfloat16
SWAP = [(p, p ^ 1) for p in range(PLACES)]
TURN = [[(p, (p + 2 * d) % PLACES) for p in range(PLACES)] for d in range(CHIPS)]


def dot_nt(a, b):
    return lax.dot_general(a, b, NT_DIMS, preferred_element_type=F32)


def block_of(shape, *lead):
    return pl.BlockSpec(shape, lambda i: tuple(lead) + (0,) * (len(shape) - len(lead)))


def probe_rows(place, rhs):
    probe = lax.broadcasted_iota(jnp.int32, (BLOCK, rhs.shape[1]), 1)
    mine = lax.broadcasted_iota(jnp.int32, (BLOCK, rhs.shape[1]), 0) + place * BLOCK
    return dot_nt((probe == mine).astype(BF16), rhs)


def spread_out(result, spread):
    rounded = result.astype(BF16)
    for copy in range(spread.shape[0]):
        spread[copy] = rounded


def call(kernel, name, shapes, in_specs, out_specs, args, scratch=(), flops=0, moved=0):
    return pl.pallas_call(
        kernel,
        grid=(1,),
        out_shape=tuple(jax.ShapeDtypeStruct(s, t) for s, t in shapes),
        in_specs=in_specs,
        out_specs=tuple(out_specs),
        scratch_shapes=list(scratch),
        cost_estimate=pl.CostEstimate(flops=flops, bytes_accessed=moved, transcendentals=0),
        compiler_params=pltpu.CompilerParams(vmem_limit_bytes=VMEM_BYTES),
        name=name,
    )(*args)


def first_kernel(place, rhs, dinv, answer, spread):
    residual = probe_rows(place[0], rhs[0]).astype(BF16)
    result = dot_nt(residual, dinv[0])
    answer[...] = result
    spread_out(result, spread)


def first_call(place, rhs, dinv):
    return call(
        first_kernel,
        "level0",
        [((BLOCK, SIZE), F32), ((NT, BLOCK, SIZE), BF16)],
        [SMEM, block_of((1, SIZE, SIZE), 0), block_of((1, SIZE, SIZE), 0)],
        [block_of((BLOCK, SIZE)), block_of((NT, BLOCK, SIZE))],
        (place, rhs, dinv),
        moved=2**22,
    )


def masked(block, alive):
    return jnp.where(alive, block, jnp.zeros_like(block))


def pick_kernel(pairs, place, here, there, known, *outs):
    mine = lax.rem(place[0], 2)
    for step in range(CHIPS):
        turn = (CHIPS - step) % CHIPS
        for core in range(2):
            for n, pair in enumerate(pairs):
                for slot in range(SLOTS):
                    at = jnp.where(mine == core, here[turn, slot, pair], there[turn, slot, pair])
                    outs[step][n, core * SLOTS + slot] = known[at]


def pick_call(name, pairs, place, here, there, known):
    shape = (len(pairs), 2 * SLOTS, BLOCK, SIZE)
    return call(
        functools.partial(pick_kernel, pairs),
        name,
        [(shape, BF16)] * CHIPS,
        [SMEM, SMEM, SMEM, block_of((NT, BLOCK, SIZE))],
        [block_of(shape)] * CHIPS,
        (place, here, there, known),
        moved=2**21,
    )


def partial_kernel(pairs, kept, place, live, *refs):
    refs = list(refs)
    got = [refs.pop(0) for _ in range(CHIPS)]
    before = [refs.pop(0) for _ in range(CHIPS)] if kept else []
    tiles = [(refs.pop(0), refs.pop(0)) for _ in pairs]
    chip, core = lax.div(place[0], 2), lax.rem(place[0], 2)
    for n, pair in enumerate(pairs):
        total = jnp.zeros((CHIPS * BLOCK, SIZE), F32)
        for swapped in range(2):
            side = lax.rem(core + swapped, 2)
            for slot in range(SLOTS):
                at = side * SLOTS + slot
                block = jnp.concatenate([g[n, at] for g in got])
                block = masked(block, chip * 2 * SLOTS + at < live[0, pair])
                total = total + dot_nt(block, tiles[n][swapped][0, slot])
        for step in range(CHIPS):
            sums = total[step * BLOCK : (step + 1) * BLOCK]
            refs[n * CHIPS + step][...] = sums + before[step][...] if kept else sums


def partial_call(name, pairs, place, live, got, kept, tiles, swapped):
    shape = (BLOCK, SIZE)
    args = [place, live, *got, *kept]
    specs = [SMEM, SMEM] + [block_of(g.shape) for g in args[2:]]
    for pair in pairs:
        args += [tiles, swapped]
        specs += [block_of((1, SLOTS, SIZE, SIZE), pair)] * 2
    return call(
        functools.partial(partial_kernel, pairs, bool(kept)),
        name,
        [(shape, F32)] * (CHIPS * len(pairs)),
        specs,
        [block_of(shape)] * (CHIPS * len(pairs)),
        args,
        flops=2 * 6 * SIZE**3,
        moved=2**21,
    )


def level_kernel(pair, index, begin, finish, returned, earlier, place, here, there, live, start, dinv, known, tiles, *refs):
    refs = list(refs)
    back = [refs.pop(0) for _ in range(returned)]
    before = [refs.pop(0) for _ in range(earlier)]
    held, sems = refs[-2:]
    chip, core = lax.div(place[0], 2), lax.rem(place[0], 2)
    chips = [lax.rem(chip + CHIPS - d, CHIPS) for d in range(CHIPS)]
    copies = [
        pltpu.make_async_copy(tiles.at[pl.ds(2 * chips[d], 2), index], held.at[pl.ds(2 * d, 2)], sems.at[d]) for d in range(CHIPS)
    ]
    for copy in copies:
        copy.start()
    total = probe_rows(place[0], start[0]) if begin else start[...]
    for sums in back:
        total = total - sums[...]
    for d in range(CHIPS):
        copies[d].wait()
        for cols, side in ((here, core), (there, 1 - core)):
            first = (2 * chips[d] + side) * SLOTS
            for slot in range(SLOTS):
                block = masked(known[cols[d, slot, pair]], first + slot < live[0, pair])
                total = total - dot_nt(block, held[2 * d + side, slot * SIZE : (slot + 1) * SIZE])
    if not finish:
        refs[0][...] = total
        return
    result = dot_nt(total.astype(BF16), dinv[0])
    if earlier:
        for n in range(earlier):
            refs[0][n] = before[n][...]
        refs[0][earlier] = result
        return
    refs[0][...] = result
    spread_out(result, refs[1])


def level_call(name, level, pair, index, begin, finish, place, here, there, live, start, dinv, known, tiles, back, earlier):
    flat, pick = block_of((BLOCK, SIZE)), block_of((1, SIZE, SIZE), level)
    if not finish:
        shapes, outs = [((BLOCK, SIZE), F32)], [flat]
    elif earlier:
        shapes, outs = [((level + 1, BLOCK, SIZE), F32)], [block_of((level + 1, BLOCK, SIZE))]
    else:
        shapes = [((BLOCK, SIZE), F32), ((NT, BLOCK, SIZE), BF16)]
        outs = [flat, block_of((NT, BLOCK, SIZE))]
    return call(
        functools.partial(level_kernel, pair, index, begin, finish, len(back), len(earlier)),
        name,
        shapes,
        [SMEM] * 4 + [pick if begin else flat, pick, block_of((NT, BLOCK, SIZE)), ANY] + [flat] * (len(back) + len(earlier)),
        outs,
        (place, here, there, live, start, dinv, known, tiles, *back, *earlier),
        [pltpu.VMEM((PLACES, SLOTS * SIZE, SIZE), BF16), pltpu.SemaphoreType.DMA((CHIPS,))],
        flops=2 * 24 * BLOCK * SIZE * SIZE,
        moved=24 * SIZE * SIZE * 2,
    )


def local(rhs, dinv, factor, cols, live):
    place = lax.axis_index("col").astype(jnp.int32).reshape(1)
    tiles = factor.transpose(0, 2, 1, 3)
    move = lambda array, pairs: lax.ppermute(array, "col", pairs)
    over_row = lambda array: lax.all_to_all(array, "row", 0, 0, tiled=True)

    gather = lambda array: lax.all_gather(array, "col", axis=0, tiled=False)
    live = live.transpose(1, 0)

    own = cols.transpose(2, 1, 0).reshape(SLOTS, -1)
    here = jnp.stack([own] + [move(own, TURN[d]) for d in range(1, CHIPS)])
    there = move(here, SWAP)
    answer0, spread0 = first_call(place, rhs, dinv)
    gathered02 = gather(tiles[0:3:2].reshape(2, SLOTS * SIZE, SIZE))

    def send(picked):
        return [picked[0]] + [move(picked[d], TURN[d]) for d in range(1, CHIPS)]

    def give_back(sums):
        return [sums[0]] + [move(sums[d], TURN[CHIPS - d]) for d in range(1, CHIPS)]

    scalars = (place, here, there, live)
    known0 = over_row(spread0)
    picked = pick_call("pick13", (1, 3), place, here, there, known0)
    later, known0, *picked = lax.optimization_barrier((tiles, known0, *picked))
    gathered45 = gather(later[4:6].reshape(2, SLOTS * SIZE, SIZE))
    swapped = move(later, SWAP)
    got = send(picked)
    answer1, spread1 = level_call("level1", 1, 0, 0, True, True, *scalars, rhs, dinv, known0, gathered02, [], [])
    spread1, *got = lax.optimization_barrier((spread1, *got))
    known1 = over_row(spread1)

    sums = partial_call("partial13", (1, 3), place, live, got, [], tiles, swapped)
    back2, back3 = give_back(sums[:CHIPS]), give_back(sums[CHIPS:])
    answer2, spread2 = level_call("level2", 2, 2, 1, True, True, *scalars, rhs, dinv, known1, gathered02, back2, [])
    known2 = over_row(spread2)
    (early3,) = level_call("early3", 3, 4, 0, True, False, *scalars, rhs, dinv, known1, gathered45, back3, [])
    (solved,) = level_call(
        "level3", 3, 5, 1, False, True, *scalars, early3, dinv, known2, gathered45, [], [answer0, answer1, answer2]
    )
    return solved.transpose(0, 2, 1)


def solution(mesh):
    in_specs = (
        P(None, "row", None),
        P(None, "row", None),
        P(None, "row", "col", None),
        P(None, "row", "col"),
        P(None, "row"),
    )
    out_specs = P(None, "row", "col")
    return jax.shard_map(local, mesh=mesh, in_specs=in_specs, out_specs=out_specs, check_vma=False)
```

```python
import functools

import jax
import jax.numpy as jnp
from jax import lax
from jax.experimental import pallas as pl
from jax.experimental.pallas import tpu as pltpu
from jax.sharding import PartitionSpec as P

NT_DIMS = (((1,), (1,)), ((), ()))
BLOCK = 32
SIZE = 256
SLOTS = 3
PLACES = 8
CHIPS = 4
NT = 32
VMEM_BYTES = 56 * 1024 * 1024
SMEM = pl.BlockSpec(memory_space=pltpu.SMEM)
ANY = pl.BlockSpec(memory_space=pl.ANY)
F32, BF16 = jnp.float32, jnp.bfloat16
SWAP = [(p, p ^ 1) for p in range(PLACES)]
TURN = [[(p, (p + 2 * d) % PLACES) for p in range(PLACES)] for d in range(CHIPS)]


def dot_nt(a, b):
    return lax.dot_general(a, b, NT_DIMS, preferred_element_type=F32)


def block_of(shape, *lead):
    return pl.BlockSpec(shape, lambda i: tuple(lead) + (0,) * (len(shape) - len(lead)))


def probe_rows(place, rhs):
    probe = lax.broadcasted_iota(jnp.int32, (BLOCK, rhs.shape[1]), 1)
    mine = lax.broadcasted_iota(jnp.int32, (BLOCK, rhs.shape[1]), 0) + place * BLOCK
    return dot_nt((probe == mine).astype(BF16), rhs)


def spread_out(result, spread):
    rounded = result.astype(BF16)
    for copy in range(spread.shape[0]):
        spread[copy] = rounded


def call(kernel, name, shapes, in_specs, out_specs, args, scratch=(), flops=0, moved=0):
    return pl.pallas_call(
        kernel,
        grid=(1,),
        out_shape=tuple(jax.ShapeDtypeStruct(s, t) for s, t in shapes),
        in_specs=in_specs,
        out_specs=tuple(out_specs),
        scratch_shapes=list(scratch),
        cost_estimate=pl.CostEstimate(flops=flops, bytes_accessed=moved, transcendentals=0),
        compiler_params=pltpu.CompilerParams(vmem_limit_bytes=VMEM_BYTES),
        name=name,
    )(*args)


def first_kernel(place, rhs, dinv, *refs):
    tiles, answer, spread, cuts = refs[:4], refs[4], refs[5], refs[6:]
    residual = probe_rows(place[0], rhs[0]).astype(BF16)
    result = dot_nt(residual, dinv[0])
    answer[...] = result
    spread_out(result, spread)
    for n in range(4):
        for slot in range(SLOTS):
            cuts[n // 2][n % 2, slot * SIZE : (slot + 1) * SIZE] = tiles[n][0, slot]


def first_call(place, rhs, dinv, tiles, pairs):
    diag, cut = block_of((1, SIZE, SIZE), 0), (2, SLOTS * SIZE, SIZE)
    return call(
        first_kernel,
        "level0",
        [((BLOCK, SIZE), F32), ((NT, BLOCK, SIZE), BF16), (cut, BF16), (cut, BF16)],
        [SMEM, diag, diag] + [block_of((1, SLOTS, SIZE, SIZE), p) for p in pairs],
        [block_of((BLOCK, SIZE)), block_of((NT, BLOCK, SIZE)), block_of(cut), block_of(cut)],
        (place, rhs, dinv) + (tiles,) * 4,
        moved=2**22,
    )


def solve_kernel(place, rhs, dinv, *refs):
    total = probe_rows(place[0], rhs[0])
    for sums in refs[:CHIPS]:
        total = total - sums[...]
    result = dot_nt(total.astype(BF16), dinv[0])
    refs[CHIPS][...] = result
    spread_out(result, refs[CHIPS + 1])


def solve_call(name, level, place, rhs, dinv, back):
    diag, flat = block_of((1, SIZE, SIZE), level), block_of((BLOCK, SIZE))
    return call(
        solve_kernel,
        name,
        [((BLOCK, SIZE), F32), ((NT, BLOCK, SIZE), BF16)],
        [SMEM, diag, diag] + [flat] * CHIPS,
        [flat, block_of((NT, BLOCK, SIZE))],
        (place, rhs, dinv, *back),
        moved=2**20,
    )


def masked(block, alive):
    return jnp.where(alive, block, jnp.zeros_like(block))


def pick_kernel(pairs, place, here, there, known, *outs):
    mine = lax.rem(place[0], 2)
    for step in range(CHIPS):
        turn = (CHIPS - step) % CHIPS
        for core in range(2):
            for n, pair in enumerate(pairs):
                for slot in range(SLOTS):
                    at = jnp.where(mine == core, here[turn, slot, pair], there[turn, slot, pair])
                    outs[step][n, core * SLOTS + slot] = known[at]


def pick_call(name, pairs, place, here, there, known):
    shape = (len(pairs), 2 * SLOTS, BLOCK, SIZE)
    return call(
        functools.partial(pick_kernel, pairs),
        name,
        [(shape, BF16)] * CHIPS,
        [SMEM, SMEM, SMEM, block_of((NT, BLOCK, SIZE))],
        [block_of(shape)] * CHIPS,
        (place, here, there, known),
        moved=2**21,
    )


def partial_kernel(pairs, kept, place, live, *refs):
    refs = list(refs)
    got = [refs.pop(0) for _ in range(CHIPS)]
    before = [refs.pop(0) for _ in range(CHIPS)] if kept else []
    tiles = [(refs.pop(0), refs.pop(0)) for _ in pairs]
    chip, core = lax.div(place[0], 2), lax.rem(place[0], 2)
    for n, pair in enumerate(pairs):
        total = jnp.zeros((CHIPS * BLOCK, SIZE), F32)
        for swapped in range(2):
            side = lax.rem(core + swapped, 2)
            for slot in range(SLOTS):
                at = side * SLOTS + slot
                block = jnp.concatenate([g[n, at] for g in got])
                block = masked(block, chip * 2 * SLOTS + at < live[0, pair])
                total = total + dot_nt(block, tiles[n][swapped][0, slot])
        for step in range(CHIPS):
            sums = total[step * BLOCK : (step + 1) * BLOCK]
            refs[n * CHIPS + step][...] = sums + before[step][...] if kept else sums


def partial_call(name, pairs, place, live, got, kept, tiles, swapped):
    shape = (BLOCK, SIZE)
    args = [place, live, *got, *kept]
    specs = [SMEM, SMEM] + [block_of(g.shape) for g in args[2:]]
    for pair in pairs:
        args += [tiles, swapped]
        specs += [block_of((1, SLOTS, SIZE, SIZE), pair)] * 2
    return call(
        functools.partial(partial_kernel, pairs, bool(kept)),
        name,
        [(shape, F32)] * (CHIPS * len(pairs)),
        specs,
        [block_of(shape)] * (CHIPS * len(pairs)),
        args,
        flops=2 * 6 * SIZE**3,
        moved=2**21,
    )


def level_kernel(pair, index, begin, finish, returned, earlier, place, here, there, live, start, dinv, known, tiles, *refs):
    refs = list(refs)
    back = [refs.pop(0) for _ in range(returned)]
    before = [refs.pop(0) for _ in range(earlier)]
    held, sems = refs[-2:]
    chip, core = lax.div(place[0], 2), lax.rem(place[0], 2)
    chips = [lax.rem(chip + CHIPS - d, CHIPS) for d in range(CHIPS)]
    copies = [
        pltpu.make_async_copy(tiles.at[pl.ds(2 * chips[d], 2), index], held.at[pl.ds(2 * d, 2)], sems.at[d]) for d in range(CHIPS)
    ]
    for copy in copies:
        copy.start()
    total = probe_rows(place[0], start[0]) if begin else start[...]
    for sums in back:
        total = total - sums[...]
    for d in range(CHIPS):
        copies[d].wait()
        for cols, side in ((here, core), (there, 1 - core)):
            first = (2 * chips[d] + side) * SLOTS
            for slot in range(SLOTS):
                block = masked(known[cols[d, slot, pair]], first + slot < live[0, pair])
                total = total - dot_nt(block, held[2 * d + side, slot * SIZE : (slot + 1) * SIZE])
    if not finish:
        refs[0][...] = total
        return
    result = dot_nt(total.astype(BF16), dinv[0])
    if earlier:
        for n in range(earlier):
            refs[0][n] = before[n][...]
        refs[0][earlier] = result
        return
    refs[0][...] = result
    spread_out(result, refs[1])


def level_call(name, level, pair, index, begin, finish, place, here, there, live, start, dinv, known, tiles, back, earlier):
    flat, pick = block_of((BLOCK, SIZE)), block_of((1, SIZE, SIZE), level)
    if not finish:
        shapes, outs = [((BLOCK, SIZE), F32)], [flat]
    elif earlier:
        shapes, outs = [((level + 1, BLOCK, SIZE), F32)], [block_of((level + 1, BLOCK, SIZE))]
    else:
        shapes = [((BLOCK, SIZE), F32), ((NT, BLOCK, SIZE), BF16)]
        outs = [flat, block_of((NT, BLOCK, SIZE))]
    return call(
        functools.partial(level_kernel, pair, index, begin, finish, len(back), len(earlier)),
        name,
        shapes,
        [SMEM] * 4 + [pick if begin else flat, pick, block_of((NT, BLOCK, SIZE)), ANY] + [flat] * (len(back) + len(earlier)),
        outs,
        (place, here, there, live, start, dinv, known, tiles, *back, *earlier),
        [pltpu.VMEM((PLACES, SLOTS * SIZE, SIZE), BF16), pltpu.SemaphoreType.DMA((CHIPS,))],
        flops=2 * 24 * BLOCK * SIZE * SIZE,
        moved=24 * SIZE * SIZE * 2,
    )


def local(rhs, dinv, factor, cols, live):
    place = lax.axis_index("col").astype(jnp.int32).reshape(1)
    tiles = factor.transpose(0, 2, 1, 3)
    move = lambda array, pairs: lax.ppermute(array, "col", pairs)
    over_row = lambda array: lax.all_to_all(array, "row", 0, 0, tiled=True)

    gather = lambda array: lax.all_gather(array, "col", axis=0, tiled=False)
    live = live.transpose(1, 0)

    own = cols.transpose(2, 1, 0).reshape(SLOTS, -1)
    here = jnp.stack([own] + [move(own, TURN[d]) for d in range(1, CHIPS)])
    there = move(here, SWAP)
    answer0, spread0, cut12, cut45 = first_call(place, rhs, dinv, tiles, (1, 2, 4, 5))
    gathered12, gathered45 = gather(cut12), gather(cut45)

    def send(picked):
        return [picked[0]] + [move(picked[d], TURN[d]) for d in range(1, CHIPS)]

    def give_back(sums):
        return [sums[0]] + [move(sums[d], TURN[CHIPS - d]) for d in range(1, CHIPS)]

    scalars = (place, here, there, live)
    known0 = over_row(spread0)
    later, *picked = lax.optimization_barrier((tiles, *pick_call("pick0", (0,), place, here, there, known0)))
    swapped = move(later, SWAP)
    got = send(picked)
    back1 = give_back(partial_call("partial0", (0,), place, live, got, [], tiles, swapped))
    answer1, spread1 = solve_call("level1", 1, place, rhs, dinv, back1)
    known1 = over_row(spread1)

    known0, spread1 = lax.optimization_barrier((known0, spread1))
    got = send(pick_call("pick3", (3,), place, here, there, known0))
    (early2,) = level_call("early2", 2, 1, 0, True, False, *scalars, rhs, dinv, known0, gathered12, [], [])
    known1, early2, *got = lax.optimization_barrier((known1, early2, *got))
    back3 = give_back(partial_call("partial3", (3,), place, live, got, [], tiles, swapped))
    answer2, spread2 = level_call("level2", 2, 2, 1, False, True, *scalars, early2, dinv, known1, gathered12, [], [])
    known2 = over_row(spread2)
    (early3,) = level_call("early3", 3, 4, 0, True, False, *scalars, rhs, dinv, known1, gathered45, back3, [])
    (solved,) = level_call(
        "level3", 3, 5, 1, False, True, *scalars, early3, dinv, known2, gathered45, [], [answer0, answer1, answer2]
    )
    return solved.transpose(0, 2, 1)


def solution(mesh):
    in_specs = (
        P(None, "row", None),
        P(None, "row", None),
        P(None, "row", "col", None),
        P(None, "row", "col"),
        P(None, "row"),
    )
    out_specs = P(None, "row", "col")
    return jax.shard_map(local, mesh=mesh, in_specs=in_specs, out_specs=out_specs, check_vma=False)
```

```python
import functools

import jax
import jax.numpy as jnp
from jax import lax
from jax.experimental import pallas as pl
from jax.experimental.pallas import tpu as pltpu
from jax.sharding import PartitionSpec as P

NT_DIMS = (((1,), (1,)), ((), ()))
BLOCK = 32
SIZE = 256
SLOTS = 3
PLACES = 8
CHIPS = 4
NT = 32
VMEM_BYTES = 56 * 1024 * 1024
SMEM = pl.BlockSpec(memory_space=pltpu.SMEM)
ANY = pl.BlockSpec(memory_space=pl.ANY)
F32, BF16 = jnp.float32, jnp.bfloat16
SWAP = [(p, p ^ 1) for p in range(PLACES)]
SAME = [(2 * y, 2 * ((y + 1) % CHIPS)) for y in range(CHIPS)] + [
    (2 * y + 1, 2 * ((y - 1) % CHIPS) + 1) for y in range(CHIPS)
]
CROSS = [(2 * y + 1, 2 * ((y + 1) % CHIPS)) for y in range(CHIPS)] + [
    (2 * y, 2 * ((y - 1) % CHIPS) + 1) for y in range(CHIPS)
]
TURN = [[(p, (p + 2 * d) % PLACES) for p in range(PLACES)] for d in range(CHIPS)]


def dot_nt(a, b):
    return lax.dot_general(a, b, NT_DIMS, preferred_element_type=F32)


def block_of(shape, *lead):
    return pl.BlockSpec(shape, lambda i: tuple(lead) + (0,) * (len(shape) - len(lead)))


def probe_rows(place, rhs):
    probe = lax.broadcasted_iota(jnp.int32, (BLOCK, rhs.shape[1]), 1)
    mine = lax.broadcasted_iota(jnp.int32, (BLOCK, rhs.shape[1]), 0) + place * BLOCK
    return dot_nt((probe == mine).astype(BF16), rhs)


def spread_out(result, spread):
    rounded = result.astype(BF16)
    for copy in range(spread.shape[0]):
        spread[copy] = rounded


def call(kernel, name, shapes, in_specs, out_specs, args, scratch=(), flops=0, moved=0):
    return pl.pallas_call(
        kernel,
        grid=(1,),
        out_shape=tuple(jax.ShapeDtypeStruct(s, t) for s, t in shapes),
        in_specs=in_specs,
        out_specs=tuple(out_specs),
        scratch_shapes=list(scratch),
        cost_estimate=pl.CostEstimate(flops=flops, bytes_accessed=moved, transcendentals=0),
        compiler_params=pltpu.CompilerParams(vmem_limit_bytes=VMEM_BYTES),
        name=name,
    )(*args)


def first_kernel(place, rhs, dinv, *refs):
    tiles, answer, spread, cuts = refs[:4], refs[4], refs[5], refs[6:]
    residual = probe_rows(place[0], rhs[0]).astype(BF16)
    result = dot_nt(residual, dinv[0])
    answer[...] = result
    spread_out(result, spread)
    for n in range(4):
        for slot in range(SLOTS):
            cuts[min(n, 2)][max(n - 2, 0), slot * SIZE : (slot + 1) * SIZE] = tiles[n][0, slot]


def first_call(place, rhs, dinv, tiles, pairs):
    diag, cuts = block_of((1, SIZE, SIZE), 0), [(n, SLOTS * SIZE, SIZE) for n in (1, 1, 2)]
    return call(
        first_kernel,
        "level0",
        [((BLOCK, SIZE), F32), ((NT, BLOCK, SIZE), BF16)] + [(cut, BF16) for cut in cuts],
        [SMEM, diag, diag] + [block_of((1, SLOTS, SIZE, SIZE), p) for p in pairs],
        [block_of((BLOCK, SIZE)), block_of((NT, BLOCK, SIZE))] + [block_of(cut) for cut in cuts],
        (place, rhs, dinv) + (tiles,) * 4,
        moved=2**22,
    )


def masked(block, alive):
    return jnp.where(alive, block, jnp.zeros_like(block))


def pick_kernel(pairs, place, here, there, known, *outs):
    mine = lax.rem(place[0], 2)
    for step in range(CHIPS):
        turn = (CHIPS - step) % CHIPS
        for core in range(2):
            for n, pair in enumerate(pairs):
                for slot in range(SLOTS):
                    at = jnp.where(mine == core, here[turn, slot, pair], there[turn, slot, pair])
                    outs[step][n, core * SLOTS + slot] = known[at]


def pick_call(name, pairs, place, here, there, known):
    shape = (len(pairs), 2 * SLOTS, BLOCK, SIZE)
    return call(
        functools.partial(pick_kernel, pairs),
        name,
        [(shape, BF16)] * CHIPS,
        [SMEM, SMEM, SMEM, block_of((NT, BLOCK, SIZE))],
        [block_of(shape)] * CHIPS,
        (place, here, there, known),
        moved=2**21,
    )


def partial_kernel(pairs, kept, place, live, *refs):
    refs = list(refs)
    got = [refs.pop(0) for _ in range(CHIPS)]
    before = [refs.pop(0) for _ in range(CHIPS)] if kept else []
    tiles = [(refs.pop(0), refs.pop(0)) for _ in pairs]
    chip, core = lax.div(place[0], 2), lax.rem(place[0], 2)
    for n, pair in enumerate(pairs):
        total = jnp.zeros((CHIPS * BLOCK, SIZE), F32)
        for swapped in range(2):
            side = lax.rem(core + swapped, 2)
            for slot in range(SLOTS):
                at = side * SLOTS + slot
                block = jnp.concatenate([g[n, at] for g in got])
                block = masked(block, chip * 2 * SLOTS + at < live[0, pair])
                total = total + dot_nt(block, tiles[n][swapped][0, slot])
        for step in range(CHIPS):
            sums = total[step * BLOCK : (step + 1) * BLOCK]
            refs[n * CHIPS + step][...] = sums + before[step][...] if kept else sums


def partial_call(name, pairs, place, live, got, kept, tiles, swapped):
    shape = (BLOCK, SIZE)
    args = [place, live, *got, *kept]
    specs = [SMEM, SMEM] + [block_of(g.shape) for g in args[2:]]
    for pair in pairs:
        args += [tiles, swapped]
        specs += [block_of((1, SLOTS, SIZE, SIZE), pair)] * 2
    return call(
        functools.partial(partial_kernel, pairs, bool(kept)),
        name,
        [(shape, F32)] * (CHIPS * len(pairs)),
        specs,
        [block_of(shape)] * (CHIPS * len(pairs)),
        args,
        flops=2 * 6 * SIZE**3,
        moved=2**21,
    )


def level_kernel(pair, index, begin, finish, returned, earlier, place, here, there, live, start, dinv, known, tiles, *refs):
    refs = list(refs)
    back = [refs.pop(0) for _ in range(returned)]
    before = [refs.pop(0) for _ in range(earlier)]
    held, sems = refs[-2:]
    chip, core = lax.div(place[0], 2), lax.rem(place[0], 2)
    chips = [lax.rem(chip + CHIPS - d, CHIPS) for d in range(CHIPS)]
    copies = [
        pltpu.make_async_copy(tiles.at[pl.ds(2 * chips[d], 2), index], held.at[pl.ds(2 * d, 2)], sems.at[d]) for d in range(CHIPS)
    ]
    for copy in copies:
        copy.start()
    total = probe_rows(place[0], start[0]) if begin else start[...]
    for sums in back:
        total = total - sums[...]
    for d in range(CHIPS):
        copies[d].wait()
        for cols, side in ((here, core), (there, 1 - core)):
            first = (2 * chips[d] + side) * SLOTS
            for slot in range(SLOTS):
                block = masked(known[cols[d, slot, pair]], first + slot < live[0, pair])
                total = total - dot_nt(block, held[2 * d + side, slot * SIZE : (slot + 1) * SIZE])
    if not finish:
        refs[0][...] = total
        return
    result = dot_nt(total.astype(BF16), dinv[0])
    if earlier:
        for n in range(earlier):
            refs[0][n] = before[n][...]
        refs[0][earlier] = result
        return
    refs[0][...] = result
    spread_out(result, refs[1])


def level_call(name, level, pair, index, begin, finish, place, here, there, live, start, dinv, known, tiles, back, earlier):
    flat, pick = block_of((BLOCK, SIZE)), block_of((1, SIZE, SIZE), level)
    if not finish:
        shapes, outs = [((BLOCK, SIZE), F32)], [flat]
    elif earlier:
        shapes, outs = [((level + 1, BLOCK, SIZE), F32)], [block_of((level + 1, BLOCK, SIZE))]
    else:
        shapes = [((BLOCK, SIZE), F32), ((NT, BLOCK, SIZE), BF16)]
        outs = [flat, block_of((NT, BLOCK, SIZE))]
    return call(
        functools.partial(level_kernel, pair, index, begin, finish, len(back), len(earlier)),
        name,
        shapes,
        [SMEM] * 4 + [pick if begin else flat, pick, block_of((NT, BLOCK, SIZE)), ANY] + [flat] * (len(back) + len(earlier)),
        outs,
        (place, here, there, live, start, dinv, known, tiles, *back, *earlier),
        [pltpu.VMEM((PLACES, SLOTS * SIZE, SIZE), BF16), pltpu.SemaphoreType.DMA((CHIPS,))],
        flops=2 * 24 * BLOCK * SIZE * SIZE,
        moved=24 * SIZE * SIZE * 2,
    )


def pieces_kernel(pair, returned, place, here, there, live, rhs, dinv, known, *refs):
    refs = list(refs)
    back = [refs.pop(0) for _ in range(returned)]
    sources = [refs.pop(0) for _ in range(PLACES)]
    answer, spread, held, sems = refs
    sources = [s.at[pair] if s.shape[0] > 1 else s.at[0] for s in sources]
    copies = [pltpu.make_async_copy(sources[n], held.at[n], sems.at[n]) for n in range(PLACES)]
    for copy in copies:
        copy.start()
    total = probe_rows(place[0], rhs[0])
    for sums in back:
        total = total - sums[...]
    chip, core = lax.div(place[0], 2), lax.rem(place[0], 2)
    near, other = 1 + 2 * core, 3 - 2 * core
    kinds = [(0, 0), (near, 0), (near, 1), (2, 0), (0, 1), (other, 1), (other, 0), (2, 1)]
    for n, (turn, side) in enumerate(kinds):
        copies[n].wait()
        cols = there if side else here
        owner = 2 * lax.rem(chip + CHIPS - turn, CHIPS) + (1 - core if side else core)
        for slot in range(SLOTS):
            block = masked(known[cols[turn, slot, pair]], owner * SLOTS + slot < live[0, pair])
            total = total - dot_nt(block, held[n, slot])
    result = dot_nt(total.astype(BF16), dinv[0])
    answer[...] = result
    spread_out(result, spread)


def pieces_call(name, level, pair, place, here, there, live, rhs, dinv, known, back, sources):
    flat, diag = block_of((BLOCK, SIZE)), block_of((1, SIZE, SIZE), level)
    return call(
        functools.partial(pieces_kernel, pair, len(back)),
        name,
        [((BLOCK, SIZE), F32), ((NT, BLOCK, SIZE), BF16)],
        [SMEM] * 4 + [diag, diag, block_of((NT, BLOCK, SIZE))] + [flat] * len(back) + [ANY] * PLACES,
        [flat, block_of((NT, BLOCK, SIZE))],
        (place, here, there, live, rhs, dinv, known, *back, *sources),
        [pltpu.VMEM((PLACES, SLOTS, SIZE, SIZE), BF16), pltpu.SemaphoreType.DMA((PLACES,))],
        flops=2 * 24 * BLOCK * SIZE * SIZE,
        moved=24 * SIZE * SIZE * 2,
    )


def local(rhs, dinv, factor, cols, live):
    place = lax.axis_index("col").astype(jnp.int32).reshape(1)
    tiles = factor.transpose(0, 2, 1, 3)
    move = lambda array, pairs: lax.ppermute(array, "col", pairs)
    over_row = lambda array: lax.all_to_all(array, "row", 0, 0, tiled=True)

    gather = lambda array: lax.all_gather(array, "col", axis=0, tiled=False)
    live = live.transpose(1, 0)

    own = cols.transpose(2, 1, 0).reshape(SLOTS, -1)
    here = jnp.stack([own] + [move(own, TURN[d]) for d in range(1, CHIPS)])
    there = move(here, SWAP)
    answer0, spread0, cut0, cut2, cut45 = first_call(place, rhs, dinv, tiles, (0, 2, 4, 5))
    gathered0, gathered45 = gather(cut0), gather(cut45)
    cut2 = cut2.reshape(1, SLOTS, SIZE, SIZE)
    same, cross = move(cut2, SAME), move(cut2, CROSS)

    def send(picked):
        return [picked[0]] + [move(picked[d], TURN[d]) for d in range(1, CHIPS)]

    def give_back(sums):
        return [sums[0]] + [move(sums[d], TURN[CHIPS - d]) for d in range(1, CHIPS)]

    scalars = (place, here, there, live)
    known0 = over_row(spread0)
    known0, same, cross = lax.optimization_barrier((known0, same, cross))
    picked = pick_call("pick13", (1, 3), place, here, there, known0)
    later, known0, *picked = lax.optimization_barrier((tiles, known0, *picked))
    swapped = move(later, SWAP)
    got = send(picked)
    far = move(same, SAME)
    answer1, spread1 = level_call("level1", 1, 0, 0, True, True, *scalars, rhs, dinv, known0, gathered0, [], [])
    spread1, far, *got = lax.optimization_barrier((spread1, far, *got))
    known1 = over_row(spread1)

    sums = partial_call("partial13", (1, 3), place, live, got, [], tiles, swapped)
    back2, back3 = give_back(sums[:CHIPS]), give_back(sums[CHIPS:])
    near = [same, cross, far]
    sources = [tiles] + near + [swapped] + [move(a, SWAP) for a in near]
    answer2, spread2 = pieces_call("level2", 2, 2, *scalars, rhs, dinv, known1, back2, sources)
    known2 = over_row(spread2)
    (early3,) = level_call("early3", 3, 4, 0, True, False, *scalars, rhs, dinv, known1, gathered45, back3, [])
    (solved,) = level_call(
        "level3", 3, 5, 1, False, True, *scalars, early3, dinv, known2, gathered45, [], [answer0, answer1, answer2]
    )
    return solved.transpose(0, 2, 1)


def solution(mesh):
    in_specs = (
        P(None, "row", None),
        P(None, "row", None),
        P(None, "row", "col", None),
        P(None, "row", "col"),
        P(None, "row"),
    )
    out_specs = P(None, "row", "col")
    return jax.shard_map(local, mesh=mesh, in_specs=in_specs, out_specs=out_specs, check_vma=False)
```

```python
import functools

import jax
import jax.numpy as jnp
from jax import lax
from jax.experimental import pallas as pl
from jax.experimental.pallas import tpu as pltpu
from jax.sharding import PartitionSpec as P

NT_DIMS = (((1,), (1,)), ((), ()))
BLOCK = 32
SIZE = 256
SLOTS = 3
PLACES = 8
CHIPS = 4
NT = 32
VMEM_BYTES = 56 * 1024 * 1024
SMEM = pl.BlockSpec(memory_space=pltpu.SMEM)
ANY = pl.BlockSpec(memory_space=pl.ANY)
F32, BF16 = jnp.float32, jnp.bfloat16
SWAP = [(p, p ^ 1) for p in range(PLACES)]
SAME = [(2 * y, 2 * ((y + 1) % CHIPS)) for y in range(CHIPS)] + [
    (2 * y + 1, 2 * ((y - 1) % CHIPS) + 1) for y in range(CHIPS)
]
CROSS = [(2 * y + 1, 2 * ((y + 1) % CHIPS)) for y in range(CHIPS)] + [
    (2 * y, 2 * ((y - 1) % CHIPS) + 1) for y in range(CHIPS)
]
TURN = [[(p, (p + 2 * d) % PLACES) for p in range(PLACES)] for d in range(CHIPS)]


def dot_nt(a, b):
    return lax.dot_general(a, b, NT_DIMS, preferred_element_type=F32)


def block_of(shape, *lead):
    return pl.BlockSpec(shape, lambda i: tuple(lead) + (0,) * (len(shape) - len(lead)))


def probe_rows(place, rhs):
    probe = lax.broadcasted_iota(jnp.int32, (BLOCK, rhs.shape[1]), 1)
    mine = lax.broadcasted_iota(jnp.int32, (BLOCK, rhs.shape[1]), 0) + place * BLOCK
    return dot_nt((probe == mine).astype(BF16), rhs)


def spread_out(result, spread):
    rounded = result.astype(BF16)
    for copy in range(spread.shape[0]):
        spread[copy] = rounded


def call(kernel, name, shapes, in_specs, out_specs, args, scratch=(), flops=0, moved=0):
    return pl.pallas_call(
        kernel,
        grid=(1,),
        out_shape=tuple(jax.ShapeDtypeStruct(s, t) for s, t in shapes),
        in_specs=in_specs,
        out_specs=tuple(out_specs),
        scratch_shapes=list(scratch),
        cost_estimate=pl.CostEstimate(flops=flops, bytes_accessed=moved, transcendentals=0),
        compiler_params=pltpu.CompilerParams(vmem_limit_bytes=VMEM_BYTES),
        name=name,
    )(*args)


def first_kernel(place, rhs, dinv, *refs):
    tiles, answer, spread, cuts = refs[:4], refs[4], refs[5], refs[6:]
    residual = probe_rows(place[0], rhs[0]).astype(BF16)
    result = dot_nt(residual, dinv[0])
    answer[...] = result
    spread_out(result, spread)
    for n in range(4):
        for slot in range(SLOTS):
            cuts[min(n, 2)][max(n - 2, 0), slot * SIZE : (slot + 1) * SIZE] = tiles[n][0, slot]


def first_call(place, rhs, dinv, tiles, pairs):
    diag, cuts = block_of((1, SIZE, SIZE), 0), [(n, SLOTS * SIZE, SIZE) for n in (1, 1, 2)]
    return call(
        first_kernel,
        "level0",
        [((BLOCK, SIZE), F32), ((NT, BLOCK, SIZE), BF16)] + [(cut, BF16) for cut in cuts],
        [SMEM, diag, diag] + [block_of((1, SLOTS, SIZE, SIZE), p) for p in pairs],
        [block_of((BLOCK, SIZE)), block_of((NT, BLOCK, SIZE))] + [block_of(cut) for cut in cuts],
        (place, rhs, dinv) + (tiles,) * 4,
        moved=2**22,
    )


def masked(block, alive):
    return jnp.where(alive, block, jnp.zeros_like(block))


def pick_kernel(pairs, place, here, there, known, *outs):
    mine = lax.rem(place[0], 2)
    for step in range(CHIPS):
        turn = (CHIPS - step) % CHIPS
        for core in range(2):
            for n, pair in enumerate(pairs):
                for slot in range(SLOTS):
                    at = jnp.where(mine == core, here[turn, slot, pair], there[turn, slot, pair])
                    outs[step][n, core * SLOTS + slot] = known[at]


def pick_call(name, pairs, place, here, there, known):
    shape = (len(pairs), 2 * SLOTS, BLOCK, SIZE)
    return call(
        functools.partial(pick_kernel, pairs),
        name,
        [(shape, BF16)] * CHIPS,
        [SMEM, SMEM, SMEM, block_of((NT, BLOCK, SIZE))],
        [block_of(shape)] * CHIPS,
        (place, here, there, known),
        moved=2**21,
    )


def partial_kernel(pairs, kept, place, live, *refs):
    refs = list(refs)
    got = [refs.pop(0) for _ in range(CHIPS)]
    before = [refs.pop(0) for _ in range(CHIPS)] if kept else []
    tiles = [(refs.pop(0), refs.pop(0)) for _ in pairs]
    chip, core = lax.div(place[0], 2), lax.rem(place[0], 2)
    for n, pair in enumerate(pairs):
        total = jnp.zeros((CHIPS * BLOCK, SIZE), F32)
        for swapped in range(2):
            side = lax.rem(core + swapped, 2)
            for slot in range(SLOTS):
                at = side * SLOTS + slot
                block = jnp.concatenate([g[n, at] for g in got])
                block = masked(block, chip * 2 * SLOTS + at < live[0, pair])
                total = total + dot_nt(block, tiles[n][swapped][0, slot])
        for step in range(CHIPS):
            sums = total[step * BLOCK : (step + 1) * BLOCK]
            refs[n * CHIPS + step][...] = sums + before[step][...] if kept else sums


def partial_call(name, pairs, place, live, got, kept, tiles, swapped):
    shape = (BLOCK, SIZE)
    args = [place, live, *got, *kept]
    specs = [SMEM, SMEM] + [block_of(g.shape) for g in args[2:]]
    for pair in pairs:
        args += [tiles, swapped]
        specs += [block_of((1, SLOTS, SIZE, SIZE), pair)] * 2
    return call(
        functools.partial(partial_kernel, pairs, bool(kept)),
        name,
        [(shape, F32)] * (CHIPS * len(pairs)),
        specs,
        [block_of(shape)] * (CHIPS * len(pairs)),
        args,
        flops=2 * 6 * SIZE**3,
        moved=2**21,
    )


def level_kernel(pair, index, begin, finish, returned, earlier, place, here, there, live, start, dinv, known, tiles, *refs):
    refs = list(refs)
    back = [refs.pop(0) for _ in range(returned)]
    before = [refs.pop(0) for _ in range(earlier)]
    held, sems = refs[-2:]
    chip, core = lax.div(place[0], 2), lax.rem(place[0], 2)
    chips = [lax.rem(chip + CHIPS - d, CHIPS) for d in range(CHIPS)]
    copies = [
        pltpu.make_async_copy(tiles.at[pl.ds(2 * chips[d], 2), index], held.at[pl.ds(2 * d, 2)], sems.at[d]) for d in range(CHIPS)
    ]
    for copy in copies:
        copy.start()
    total = probe_rows(place[0], start[0]) if begin else start[...]
    for sums in back:
        total = total - sums[...]
    for d in range(CHIPS):
        copies[d].wait()
        for cols, side in ((here, core), (there, 1 - core)):
            first = (2 * chips[d] + side) * SLOTS
            for slot in range(SLOTS):
                block = masked(known[cols[d, slot, pair]], first + slot < live[0, pair])
                total = total - dot_nt(block, held[2 * d + side, slot * SIZE : (slot + 1) * SIZE])
    if not finish:
        refs[0][...] = total
        return
    result = dot_nt(total.astype(BF16), dinv[0])
    if earlier:
        for n in range(earlier):
            refs[0][n] = before[n][...]
        refs[0][earlier] = result
        return
    refs[0][...] = result
    spread_out(result, refs[1])


def level_call(name, level, pair, index, begin, finish, place, here, there, live, start, dinv, known, tiles, back, earlier):
    flat, pick = block_of((BLOCK, SIZE)), block_of((1, SIZE, SIZE), level)
    if not finish:
        shapes, outs = [((BLOCK, SIZE), F32)], [flat]
    elif earlier:
        shapes, outs = [((level + 1, BLOCK, SIZE), F32)], [block_of((level + 1, BLOCK, SIZE))]
    else:
        shapes = [((BLOCK, SIZE), F32), ((NT, BLOCK, SIZE), BF16)]
        outs = [flat, block_of((NT, BLOCK, SIZE))]
    return call(
        functools.partial(level_kernel, pair, index, begin, finish, len(back), len(earlier)),
        name,
        shapes,
        [SMEM] * 4 + [pick if begin else flat, pick, block_of((NT, BLOCK, SIZE)), ANY] + [flat] * (len(back) + len(earlier)),
        outs,
        (place, here, there, live, start, dinv, known, tiles, *back, *earlier),
        [pltpu.VMEM((PLACES, SLOTS * SIZE, SIZE), BF16), pltpu.SemaphoreType.DMA((CHIPS,))],
        flops=2 * 24 * BLOCK * SIZE * SIZE,
        moved=24 * SIZE * SIZE * 2,
    )


def pieces_kernel(pair, returned, place, here, there, live, rhs, dinv, known, *refs):
    refs = list(refs)
    back = [refs.pop(0) for _ in range(returned)]
    sources = [refs.pop(0) for _ in range(PLACES)]
    answer, spread, held, sems = refs
    sources = [s.at[pair] if s.shape[0] > 1 else s.at[0] for s in sources]
    copies = [pltpu.make_async_copy(sources[n], held.at[n], sems.at[n]) for n in range(PLACES)]
    for copy in copies:
        copy.start()
    total = probe_rows(place[0], rhs[0])
    for sums in back:
        total = total - sums[...]
    chip, core = lax.div(place[0], 2), lax.rem(place[0], 2)
    near, other = 1 + 2 * core, 3 - 2 * core
    kinds = [(0, 0), (near, 0), (near, 1), (2, 0), (0, 1), (other, 1), (other, 0), (2, 1)]
    for n, (turn, side) in enumerate(kinds):
        copies[n].wait()
        cols = there if side else here
        owner = 2 * lax.rem(chip + CHIPS - turn, CHIPS) + (1 - core if side else core)
        for slot in range(SLOTS):
            block = masked(known[cols[turn, slot, pair]], owner * SLOTS + slot < live[0, pair])
            total = total - dot_nt(block, held[n, slot])
    result = dot_nt(total.astype(BF16), dinv[0])
    answer[...] = result
    spread_out(result, spread)


def pieces_call(name, level, pair, place, here, there, live, rhs, dinv, known, back, sources):
    flat, diag = block_of((BLOCK, SIZE)), block_of((1, SIZE, SIZE), level)
    return call(
        functools.partial(pieces_kernel, pair, len(back)),
        name,
        [((BLOCK, SIZE), F32), ((NT, BLOCK, SIZE), BF16)],
        [SMEM] * 4 + [diag, diag, block_of((NT, BLOCK, SIZE))] + [flat] * len(back) + [ANY] * PLACES,
        [flat, block_of((NT, BLOCK, SIZE))],
        (place, here, there, live, rhs, dinv, known, *back, *sources),
        [pltpu.VMEM((PLACES, SLOTS, SIZE, SIZE), BF16), pltpu.SemaphoreType.DMA((PLACES,))],
        flops=2 * 24 * BLOCK * SIZE * SIZE,
        moved=24 * SIZE * SIZE * 2,
    )


def local(rhs, dinv, factor, cols, live):
    place = lax.axis_index("col").astype(jnp.int32).reshape(1)
    tiles = factor.transpose(0, 2, 1, 3)
    move = lambda array, pairs: lax.ppermute(array, "col", pairs)
    over_row = lambda array: lax.all_to_all(array, "row", 0, 0, tiled=True)

    gather = lambda array: lax.all_gather(array, "col", axis=0, tiled=False)
    live = live.transpose(1, 0)

    own = cols.transpose(2, 1, 0).reshape(SLOTS, -1)
    turned = [move(own, TURN[d]) for d in range(1, CHIPS)]
    here = jnp.stack([own] + turned)
    there = move(here, SWAP)
    answer0, spread0, cut0, cut2, cut45 = first_call(place, rhs, dinv, tiles, (0, 2, 4, 5))
    gathered0, gathered45 = gather(cut0), gather(cut45)
    cut2, *turned = lax.optimization_barrier((cut2.reshape(1, SLOTS, SIZE, SIZE), *turned))
    same, cross = move(cut2, SAME), move(cut2, CROSS)

    def send(picked):
        return [picked[0]] + [move(picked[d], TURN[d]) for d in range(1, CHIPS)]

    def give_back(sums):
        return [sums[0]] + [move(sums[d], TURN[CHIPS - d]) for d in range(1, CHIPS)]

    scalars = (place, here, there, live)
    known0 = over_row(spread0)
    picked = pick_call("pick13", (1, 3), place, here, there, known0)
    later, known0, same, cross, *picked = lax.optimization_barrier((tiles, known0, same, cross, *picked))
    swapped = move(later, SWAP)
    got = send(picked)
    far = move(same, SAME)
    answer1, spread1 = level_call("level1", 1, 0, 0, True, True, *scalars, rhs, dinv, known0, gathered0, [], [])
    spread1, *got = lax.optimization_barrier((spread1, *got))
    known1 = over_row(spread1)

    sums = partial_call("partial13", (1, 3), place, live, got, [], tiles, swapped)
    back2, back3 = give_back(sums[:CHIPS]), give_back(sums[CHIPS:])
    near = [same, cross, far]
    sources = [tiles] + near + [swapped] + [move(a, SWAP) for a in near]
    answer2, spread2 = pieces_call("level2", 2, 2, *scalars, rhs, dinv, known1, back2, sources)
    known2 = over_row(spread2)
    (early3,) = level_call("early3", 3, 4, 0, True, False, *scalars, rhs, dinv, known1, gathered45, back3, [])
    (solved,) = level_call(
        "level3", 3, 5, 1, False, True, *scalars, early3, dinv, known2, gathered45, [], [answer0, answer1, answer2]
    )
    return solved.transpose(0, 2, 1)


def solution(mesh):
    in_specs = (
        P(None, "row", None),
        P(None, "row", None),
        P(None, "row", "col", None),
        P(None, "row", "col"),
        P(None, "row"),
    )
    out_specs = P(None, "row", "col")
    return jax.shard_map(local, mesh=mesh, in_specs=in_specs, out_specs=out_specs, check_vma=False)
```

```python
import functools

import jax
import jax.numpy as jnp
from jax import lax
from jax.experimental import pallas as pl
from jax.experimental.pallas import tpu as pltpu
from jax.sharding import PartitionSpec as P

NT_DIMS = (((1,), (1,)), ((), ()))
BLOCK = 32
SIZE = 256
SLOTS = 3
PLACES = 8
CHIPS = 4
NT = 32
VMEM_BYTES = 64 * 1024 * 1024
SMEM = pl.BlockSpec(memory_space=pltpu.SMEM)
ANY = pl.BlockSpec(memory_space=pl.ANY)
F32, BF16 = jnp.float32, jnp.bfloat16
SWAP = [(p, p ^ 1) for p in range(PLACES)]
TURN = [[(p, (p + 2 * d) % PLACES) for p in range(PLACES)] for d in range(CHIPS)]


def dot_nt(a, b):
    return lax.dot_general(a, b, NT_DIMS, preferred_element_type=F32)


def block_of(shape, *lead):
    return pl.BlockSpec(shape, lambda i: tuple(lead) + (0,) * (len(shape) - len(lead)))


def probe_rows(place, rhs):
    probe = lax.broadcasted_iota(jnp.int32, (BLOCK, rhs.shape[1]), 1)
    mine = lax.broadcasted_iota(jnp.int32, (BLOCK, rhs.shape[1]), 0) + place * BLOCK
    return dot_nt((probe == mine).astype(BF16), rhs)


def spread_out(result, spread):
    rounded = result.astype(BF16)
    for copy in range(spread.shape[0]):
        spread[copy] = rounded


def call(kernel, name, shapes, in_specs, out_specs, args, scratch=(), flops=0, moved=0):
    return pl.pallas_call(
        kernel,
        grid=(1,),
        out_shape=tuple(jax.ShapeDtypeStruct(s, t) for s, t in shapes),
        in_specs=in_specs,
        out_specs=tuple(out_specs),
        scratch_shapes=list(scratch),
        cost_estimate=pl.CostEstimate(flops=flops, bytes_accessed=moved, transcendentals=0),
        compiler_params=pltpu.CompilerParams(vmem_limit_bytes=VMEM_BYTES),
        name=name,
    )(*args)


def first_kernel(place, rhs, dinv, *refs):
    count = (len(refs) - 2) // 2
    tiles, (answer, spread), cuts = refs[:count], refs[count : count + 2], refs[count + 2 :]
    residual = probe_rows(place[0], rhs[0]).astype(BF16)
    result = dot_nt(residual, dinv[0])
    answer[...] = result
    spread_out(result, spread)
    for n in range(count):
        for slot in range(SLOTS):
            cuts[n][slot * SIZE : (slot + 1) * SIZE] = tiles[n][0, slot]


def first_call(place, rhs, dinv, tiles, pairs):
    diag, cut = block_of((1, SIZE, SIZE), 0), (SLOTS * SIZE, SIZE)
    return call(
        first_kernel,
        "level0",
        [((BLOCK, SIZE), F32), ((NT, BLOCK, SIZE), BF16)] + [(cut, BF16)] * len(pairs),
        [SMEM, diag, diag] + [block_of((1, SLOTS, SIZE, SIZE), p) for p in pairs],
        [block_of((BLOCK, SIZE)), block_of((NT, BLOCK, SIZE))] + [block_of(cut)] * len(pairs),
        (place, rhs, dinv) + (tiles,) * len(pairs),
        moved=2**22,
    )


def masked(block, alive):
    return jnp.where(alive, block, jnp.zeros_like(block))


def pick_kernel(pairs, place, here, there, known, *outs):
    mine = lax.rem(place[0], 2)
    for step in range(CHIPS):
        turn = (CHIPS - step) % CHIPS
        for core in range(2):
            for n, pair in enumerate(pairs):
                for slot in range(SLOTS):
                    at = jnp.where(mine == core, here[turn, slot, pair], there[turn, slot, pair])
                    outs[step][n, core * SLOTS + slot] = known[at]


def pick_call(name, pairs, place, here, there, known):
    shape = (len(pairs), 2 * SLOTS, BLOCK, SIZE)
    return call(
        functools.partial(pick_kernel, pairs),
        name,
        [(shape, BF16)] * CHIPS,
        [SMEM, SMEM, SMEM, block_of((NT, BLOCK, SIZE))],
        [block_of(shape)] * CHIPS,
        (place, here, there, known),
        moved=2**21,
    )


def partial_kernel(pairs, kept, place, live, *refs):
    refs = list(refs)
    got = [refs.pop(0) for _ in range(CHIPS)]
    before = [refs.pop(0) for _ in range(CHIPS)] if kept else []
    tiles = [(refs.pop(0), refs.pop(0)) for _ in pairs]
    chip, core = lax.div(place[0], 2), lax.rem(place[0], 2)
    for n, pair in enumerate(pairs):
        total = jnp.zeros((CHIPS * BLOCK, SIZE), F32)
        for swapped in range(2):
            side = lax.rem(core + swapped, 2)
            for slot in range(SLOTS):
                at = side * SLOTS + slot
                block = jnp.concatenate([g[n, at] for g in got])
                block = masked(block, chip * 2 * SLOTS + at < live[0, pair])
                total = total + dot_nt(block, tiles[n][swapped][0, slot])
        for step in range(CHIPS):
            sums = total[step * BLOCK : (step + 1) * BLOCK]
            refs[n * CHIPS + step][...] = sums + before[step][...] if kept else sums


def partial_call(name, pairs, place, live, got, kept, tiles, swapped):
    shape = (BLOCK, SIZE)
    args = [place, live, *got, *kept]
    specs = [SMEM, SMEM] + [block_of(g.shape) for g in args[2:]]
    for pair in pairs:
        args += [tiles, swapped]
        specs += [block_of((1, SLOTS, SIZE, SIZE), pair)] * 2
    return call(
        functools.partial(partial_kernel, pairs, bool(kept)),
        name,
        [(shape, F32)] * (CHIPS * len(pairs)),
        specs,
        [block_of(shape)] * (CHIPS * len(pairs)),
        args,
        flops=2 * 6 * SIZE**3,
        moved=2**21,
    )


def level_kernel(pair, returned, earlier, place, here, there, live, rhs, dinv, known, tiles, *refs):
    refs = list(refs)
    back = [refs.pop(0) for _ in range(returned)]
    before = [refs.pop(0) for _ in range(earlier)]
    held, sems = refs[-2:]
    chip, core = lax.div(place[0], 2), lax.rem(place[0], 2)
    chips = [lax.rem(chip + CHIPS - d, CHIPS) for d in range(CHIPS)]
    copies = [
        pltpu.make_async_copy(tiles.at[pl.ds(2 * chips[d], 2)], held.at[pl.ds(2 * d, 2)], sems.at[d]) for d in range(CHIPS)
    ]
    for copy in copies:
        copy.start()
    total = probe_rows(place[0], rhs[0])
    for sums in back:
        total = total - sums[...]
    for d in range(CHIPS):
        copies[d].wait()
        for cols, side in ((here, core), (there, 1 - core)):
            first = (2 * chips[d] + side) * SLOTS
            for slot in range(SLOTS):
                block = masked(known[cols[d, slot, pair]], first + slot < live[0, pair])
                total = total - dot_nt(block, held[2 * d + side, slot * SIZE : (slot + 1) * SIZE])
    result = dot_nt(total.astype(BF16), dinv[0])
    if earlier:
        for n in range(earlier):
            refs[0][n] = before[n][...]
        refs[0][earlier] = result
        return
    refs[0][...] = result
    spread_out(result, refs[1])


def level_call(level, pair, place, here, there, live, rhs, dinv, known, tiles, back, earlier):
    flat, pick = block_of((BLOCK, SIZE)), block_of((1, SIZE, SIZE), level)
    if earlier:
        shapes, outs = [((level + 1, BLOCK, SIZE), F32)], [block_of((level + 1, BLOCK, SIZE))]
    else:
        shapes = [((BLOCK, SIZE), F32), ((NT, BLOCK, SIZE), BF16)]
        outs = [flat, block_of((NT, BLOCK, SIZE))]
    return call(
        functools.partial(level_kernel, pair, len(back), len(earlier)),
        "level%d" % level,
        shapes,
        [SMEM] * 4 + [pick, pick, block_of((NT, BLOCK, SIZE)), ANY] + [flat] * (len(back) + len(earlier)),
        outs,
        (place, here, there, live, rhs, dinv, known, tiles, *back, *earlier),
        [pltpu.VMEM((PLACES, SLOTS * SIZE, SIZE), BF16), pltpu.SemaphoreType.DMA((CHIPS,))],
        flops=2 * 24 * BLOCK * SIZE * SIZE,
        moved=24 * SIZE * SIZE * 2,
    )


def local(rhs, dinv, factor, cols, live):
    place = lax.axis_index("col").astype(jnp.int32).reshape(1)
    tiles = factor.transpose(0, 2, 1, 3)
    move = lambda array, pairs: lax.ppermute(array, "col", pairs)
    over_row = lambda array: lax.all_to_all(array, "row", 0, 0, tiled=True)

    gather = lambda array: lax.all_gather(array, "col", axis=0, tiled=False)
    live = live.transpose(1, 0)

    own = cols.transpose(2, 1, 0).reshape(SLOTS, -1)
    here = jnp.stack([own] + [move(own, TURN[d]) for d in range(1, CHIPS)])
    there = move(here, SWAP)
    answer0, spread0, *cuts = first_call(place, rhs, dinv, tiles, (0, 2, 5))
    gathered0, gathered2, gathered5 = [gather(cut) for cut in cuts]

    def send(picked):
        return [picked[0]] + [move(picked[d], TURN[d]) for d in range(1, CHIPS)]

    def give_back(sums):
        return [sums[0]] + [move(sums[d], TURN[CHIPS - d]) for d in range(1, CHIPS)]

    known0 = over_row(spread0)
    picked = pick_call("pick13", (1, 3), place, here, there, known0)
    later, known0, *picked = lax.optimization_barrier((tiles, known0, *picked))
    swapped = move(later, SWAP)
    got = send(picked)
    answer1, spread1 = level_call(1, 0, place, here, there, live, rhs, dinv, known0, gathered0, [], [])
    spread1, *got = lax.optimization_barrier((spread1, *got))
    known1 = over_row(spread1)

    sums = partial_call("partial13", (1, 3), place, live, got, [], tiles, swapped)
    sums2, sums3 = sums[:CHIPS], sums[CHIPS:]
    back2 = give_back(sums2)
    known1, *back2 = lax.optimization_barrier((known1, *back2))
    picked = pick_call("pick4", (4,), place, here, there, known1)
    known1, *picked = lax.optimization_barrier((known1, *picked))
    got = send(picked)
    answer2, spread2 = level_call(2, 2, place, here, there, live, rhs, dinv, known1, gathered2, back2, [])
    spread2, *got = lax.optimization_barrier((spread2, *got))
    known2 = over_row(spread2)

    sums3 = partial_call("partial4", (4,), place, live, got, sums3, tiles, swapped)
    (solved,) = level_call(
        3, 5, place, here, there, live, rhs, dinv, known2, gathered5, give_back(sums3), [answer0, answer1, answer2]
    )
    return solved.transpose(0, 2, 1)


def solution(mesh):
    in_specs = (
        P(None, "row", None),
        P(None, "row", None),
        P(None, "row", "col", None),
        P(None, "row", "col"),
        P(None, "row"),
    )
    out_specs = P(None, "row", "col")
    return jax.shard_map(local, mesh=mesh, in_specs=in_specs, out_specs=out_specs, check_vma=False)
```

```python
import functools

import jax
import jax.numpy as jnp
from jax import lax
from jax.experimental import pallas as pl
from jax.experimental.pallas import tpu as pltpu
from jax.sharding import PartitionSpec as P

NT_DIMS = (((1,), (1,)), ((), ()))
BLOCK = 32
SIZE = 256
SLOTS = 3
PLACES = 8
CHIPS = 4
NT = 32
VMEM_BYTES = 64 * 1024 * 1024
SMEM = pl.BlockSpec(memory_space=pltpu.SMEM)
ANY = pl.BlockSpec(memory_space=pl.ANY)
F32, BF16 = jnp.float32, jnp.bfloat16
COL = ("chip", "core")
SWAP = [(p, p ^ 1) for p in range(PLACES)]
TURN = [[(p, (p + 2 * d) % PLACES) for p in range(PLACES)] for d in range(CHIPS)]


def dot_nt(a, b):
    return lax.dot_general(a, b, NT_DIMS, preferred_element_type=F32)


def block_of(shape, *lead):
    return pl.BlockSpec(shape, lambda i: tuple(lead) + (0,) * (len(shape) - len(lead)))


def probe_rows(place, rhs):
    probe = lax.broadcasted_iota(jnp.int32, (BLOCK, rhs.shape[1]), 1)
    mine = lax.broadcasted_iota(jnp.int32, (BLOCK, rhs.shape[1]), 0) + place * BLOCK
    return dot_nt((probe == mine).astype(BF16), rhs)


def spread_out(result, spread):
    rounded = result.astype(BF16)
    for copy in range(spread.shape[0]):
        spread[copy] = rounded


def call(kernel, name, shapes, in_specs, out_specs, args, scratch=(), flops=0, moved=0):
    return pl.pallas_call(
        kernel,
        grid=(1,),
        out_shape=tuple(jax.ShapeDtypeStruct(s, t) for s, t in shapes),
        in_specs=in_specs,
        out_specs=tuple(out_specs),
        scratch_shapes=list(scratch),
        cost_estimate=pl.CostEstimate(flops=flops, bytes_accessed=moved, transcendentals=0),
        compiler_params=pltpu.CompilerParams(vmem_limit_bytes=VMEM_BYTES),
        name=name,
    )(*args)


def first_kernel(place, rhs, dinv, *refs):
    count = (len(refs) - 2) // 2
    tiles, (answer, spread), cuts = refs[:count], refs[count : count + 2], refs[count + 2 :]
    residual = probe_rows(place[0], rhs[0]).astype(BF16)
    result = dot_nt(residual, dinv[0])
    answer[...] = result
    spread_out(result, spread)
    for n in range(count):
        for slot in range(SLOTS):
            cuts[n][slot * SIZE : (slot + 1) * SIZE] = tiles[n][0, slot]


def first_call(place, rhs, dinv, tiles, pairs):
    diag, cut = block_of((1, SIZE, SIZE), 0), (SLOTS * SIZE, SIZE)
    return call(
        first_kernel,
        "level0",
        [((BLOCK, SIZE), F32), ((NT, BLOCK, SIZE), BF16)] + [(cut, BF16)] * len(pairs),
        [SMEM, diag, diag] + [block_of((1, SLOTS, SIZE, SIZE), p) for p in pairs],
        [block_of((BLOCK, SIZE)), block_of((NT, BLOCK, SIZE))] + [block_of(cut)] * len(pairs),
        (place, rhs, dinv) + (tiles,) * len(pairs),
        moved=2**22,
    )


def masked(block, alive):
    return jnp.where(alive, block, jnp.zeros_like(block))


def pick_kernel(pairs, place, here, there, known, *outs):
    mine = lax.rem(place[0], 2)
    for step in range(CHIPS):
        turn = (CHIPS - step) % CHIPS
        for core in range(2):
            for n, pair in enumerate(pairs):
                for slot in range(SLOTS):
                    at = jnp.where(mine == core, here[turn, slot, pair], there[turn, slot, pair])
                    outs[step][n, core * SLOTS + slot] = known[at]


def pick_call(name, pairs, place, here, there, known):
    shape = (len(pairs), 2 * SLOTS, BLOCK, SIZE)
    return call(
        functools.partial(pick_kernel, pairs),
        name,
        [(shape, BF16)] * CHIPS,
        [SMEM, SMEM, SMEM, block_of((NT, BLOCK, SIZE))],
        [block_of(shape)] * CHIPS,
        (place, here, there, known),
        moved=2**21,
    )


def partial_kernel(pairs, kept, place, live, *refs):
    refs = list(refs)
    got = [refs.pop(0) for _ in range(CHIPS)]
    before = [refs.pop(0) for _ in range(CHIPS)] if kept else []
    tiles = [(refs.pop(0), refs.pop(0)) for _ in pairs]
    chip, core = lax.div(place[0], 2), lax.rem(place[0], 2)
    for n, pair in enumerate(pairs):
        total = jnp.zeros((CHIPS * BLOCK, SIZE), F32)
        for swapped in range(2):
            side = lax.rem(core + swapped, 2)
            for slot in range(SLOTS):
                at = side * SLOTS + slot
                block = jnp.concatenate([g[n, at] for g in got])
                block = masked(block, chip * 2 * SLOTS + at < live[0, pair])
                total = total + dot_nt(block, tiles[n][swapped][0, slot])
        for step in range(CHIPS):
            sums = total[step * BLOCK : (step + 1) * BLOCK]
            refs[n * CHIPS + step][...] = sums + before[step][...] if kept else sums


def partial_call(name, pairs, place, live, got, kept, tiles, swapped):
    shape = (BLOCK, SIZE)
    args = [place, live, *got, *kept]
    specs = [SMEM, SMEM] + [block_of(g.shape) for g in args[2:]]
    for pair in pairs:
        args += [tiles, swapped]
        specs += [block_of((1, SLOTS, SIZE, SIZE), pair)] * 2
    return call(
        functools.partial(partial_kernel, pairs, bool(kept)),
        name,
        [(shape, F32)] * (CHIPS * len(pairs)),
        specs,
        [block_of(shape)] * (CHIPS * len(pairs)),
        args,
        flops=2 * 6 * SIZE**3,
        moved=2**21,
    )


def level_kernel(pair, count, returned, earlier, place, here, there, live, rhs, dinv, known, *refs):
    refs = list(refs)
    tiles = [refs.pop(0) for _ in range(count)]
    back = [refs.pop(0) for _ in range(returned)]
    before = [refs.pop(0) for _ in range(earlier)]
    held, sems = refs[-2:]
    chip, core = lax.div(place[0], 2), lax.rem(place[0], 2)
    chips = [lax.rem(chip + CHIPS - d, CHIPS) for d in range(CHIPS)]
    split = count == 2
    copies = [
        [pltpu.make_async_copy(tiles[n].at[chips[d]], held.at[2 * d + n], sems.at[2 * d + n]) for n in range(2)]
        if split
        else [pltpu.make_async_copy(tiles[0].at[pl.ds(2 * chips[d], 2)], held.at[pl.ds(2 * d, 2)], sems.at[2 * d])]
        for d in range(CHIPS)
    ]
    for copy in sum(copies, []):
        copy.start()
    total = probe_rows(place[0], rhs[0])
    for sums in back:
        total = total - sums[...]
    for d in range(CHIPS):
        for copy in copies[d]:
            copy.wait()
        for n, (cols, side) in enumerate(((here, core), (there, 1 - core))):
            first = (2 * chips[d] + side) * SLOTS
            at = 2 * d + (n if split else side)
            for slot in range(SLOTS):
                block = masked(known[cols[d, slot, pair]], first + slot < live[0, pair])
                total = total - dot_nt(block, held[at, slot * SIZE : (slot + 1) * SIZE])
    result = dot_nt(total.astype(BF16), dinv[0])
    if earlier:
        for n in range(earlier):
            refs[0][n] = before[n][...]
        refs[0][earlier] = result
        return
    refs[0][...] = result
    spread_out(result, refs[1])


def level_call(level, pair, place, here, there, live, rhs, dinv, known, tiles, back, earlier):
    flat, pick = block_of((BLOCK, SIZE)), block_of((1, SIZE, SIZE), level)
    if earlier:
        shapes, outs = [((level + 1, BLOCK, SIZE), F32)], [block_of((level + 1, BLOCK, SIZE))]
    else:
        shapes = [((BLOCK, SIZE), F32), ((NT, BLOCK, SIZE), BF16)]
        outs = [flat, block_of((NT, BLOCK, SIZE))]
    return call(
        functools.partial(level_kernel, pair, len(tiles), len(back), len(earlier)),
        "level%d" % level,
        shapes,
        [SMEM] * 4 + [pick, pick, block_of((NT, BLOCK, SIZE))] + [ANY] * len(tiles) + [flat] * (len(back) + len(earlier)),
        outs,
        (place, here, there, live, rhs, dinv, known, *tiles, *back, *earlier),
        [pltpu.VMEM((PLACES, SLOTS * SIZE, SIZE), BF16), pltpu.SemaphoreType.DMA((PLACES,))],
        flops=2 * 24 * BLOCK * SIZE * SIZE,
        moved=24 * SIZE * SIZE * 2,
    )


def local(rhs, dinv, factor, cols, live):
    place = lax.axis_index(COL).astype(jnp.int32).reshape(1)
    tiles = factor.transpose(0, 2, 1, 3)
    move = lambda array, pairs: lax.ppermute(array, COL, pairs)
    over_row = lambda array: lax.all_to_all(array, "row", 0, 0, tiled=True)

    gather = lambda array, axes: lax.all_gather(array, axes, axis=0, tiled=False)
    live = live.transpose(1, 0)

    own = cols.transpose(2, 1, 0).reshape(SLOTS, -1)
    here = jnp.stack([own] + [move(own, TURN[d]) for d in range(1, CHIPS)])
    there = move(here, SWAP)
    answer0, spread0, *cuts = first_call(place, rhs, dinv, tiles, (0, 2, 5))
    gathered0, gathered2, gathered5 = gather(cuts[0], "chip"), gather(cuts[1], COL), gather(cuts[2], COL)

    def send(picked):
        return [picked[0]] + [move(picked[d], TURN[d]) for d in range(1, CHIPS)]

    def give_back(sums):
        return [sums[0]] + [move(sums[d], TURN[CHIPS - d]) for d in range(1, CHIPS)]

    known0 = over_row(spread0)
    picked = pick_call("pick13", (1, 3), place, here, there, known0)
    known0, *picked = lax.optimization_barrier((known0, *picked))
    got = send(picked)
    gathered0, _ = lax.optimization_barrier((gathered0, picked[0]))
    gathered0 = [gathered0, move(gathered0, SWAP)]
    answer1, spread1 = level_call(1, 0, place, here, there, live, rhs, dinv, known0, gathered0, [], [])
    later, spread1, *got = lax.optimization_barrier((tiles, spread1, *got))
    swapped = move(later, SWAP)
    known1 = over_row(spread1)

    sums = partial_call("partial13", (1, 3), place, live, got, [], tiles, swapped)
    sums2, sums3 = sums[:CHIPS], sums[CHIPS:]
    back2 = give_back(sums2)
    known1, *back2 = lax.optimization_barrier((known1, *back2))
    picked = pick_call("pick4", (4,), place, here, there, known1)
    known1, *picked = lax.optimization_barrier((known1, *picked))
    got = send(picked)
    answer2, spread2 = level_call(2, 2, place, here, there, live, rhs, dinv, known1, [gathered2], back2, [])
    spread2, *got = lax.optimization_barrier((spread2, *got))
    known2 = over_row(spread2)

    sums3 = partial_call("partial4", (4,), place, live, got, sums3, tiles, swapped)
    (solved,) = level_call(
        3, 5, place, here, there, live, rhs, dinv, known2, [gathered5], give_back(sums3), [answer0, answer1, answer2]
    )
    return solved.transpose(0, 2, 1)


def solution(mesh):
    rows, places = mesh.devices.shape
    mesh = jax.sharding.Mesh(mesh.devices.reshape(rows, places // 2, 2), ("row",) + COL)
    in_specs = (
        P(None, "row", None),
        P(None, "row", None),
        P(None, "row", COL, None),
        P(None, "row", COL),
        P(None, "row"),
    )
    out_specs = P(None, "row", COL)
    return jax.shard_map(local, mesh=mesh, in_specs=in_specs, out_specs=out_specs, check_vma=False)
```

```python
import functools

import jax
import jax.numpy as jnp
from jax import lax
from jax.experimental import pallas as pl
from jax.experimental.pallas import tpu as pltpu
from jax.sharding import PartitionSpec as P

NT_DIMS = (((1,), (1,)), ((), ()))
BLOCK = 32
SIZE = 256
SLOTS = 3
PLACES = 8
CHIPS = 4
NT = 32
VMEM_BYTES = 64 * 1024 * 1024
SMEM = pl.BlockSpec(memory_space=pltpu.SMEM)
ANY = pl.BlockSpec(memory_space=pl.ANY)
F32, BF16 = jnp.float32, jnp.bfloat16
COL = ("chip", "core")
SWAP = [(p, p ^ 1) for p in range(PLACES)]
TURN = [[(p, (p + 2 * d) % PLACES) for p in range(PLACES)] for d in range(CHIPS)]


def dot_nt(a, b):
    return lax.dot_general(a, b, NT_DIMS, preferred_element_type=F32)


def block_of(shape, *lead):
    return pl.BlockSpec(shape, lambda i: tuple(lead) + (0,) * (len(shape) - len(lead)))


def probe_rows(place, rhs):
    probe = lax.broadcasted_iota(jnp.int32, (BLOCK, rhs.shape[1]), 1)
    mine = lax.broadcasted_iota(jnp.int32, (BLOCK, rhs.shape[1]), 0) + place * BLOCK
    return dot_nt((probe == mine).astype(BF16), rhs)


def spread_out(result, spread):
    rounded = result.astype(BF16)
    for copy in range(spread.shape[0]):
        spread[copy] = rounded


def call(kernel, name, shapes, in_specs, out_specs, args, scratch=(), flops=0, moved=0):
    return pl.pallas_call(
        kernel,
        grid=(1,),
        out_shape=tuple(jax.ShapeDtypeStruct(s, t) for s, t in shapes),
        in_specs=in_specs,
        out_specs=tuple(out_specs),
        scratch_shapes=list(scratch),
        cost_estimate=pl.CostEstimate(flops=flops, bytes_accessed=moved, transcendentals=0),
        compiler_params=pltpu.CompilerParams(vmem_limit_bytes=VMEM_BYTES),
        name=name,
    )(*args)


def first_kernel(place, rhs, dinv, *refs):
    count = (len(refs) - 2) // 2
    tiles, (answer, spread), cuts = refs[:count], refs[count : count + 2], refs[count + 2 :]
    residual = probe_rows(place[0], rhs[0]).astype(BF16)
    result = dot_nt(residual, dinv[0])
    answer[...] = result
    spread_out(result, spread)
    for n in range(count):
        for slot in range(SLOTS):
            cuts[n][slot * SIZE : (slot + 1) * SIZE] = tiles[n][0, slot]


def first_call(place, rhs, dinv, tiles, pairs):
    diag, cut = block_of((1, SIZE, SIZE), 0), (SLOTS * SIZE, SIZE)
    return call(
        first_kernel,
        "level0",
        [((BLOCK, SIZE), F32), ((NT, BLOCK, SIZE), BF16)] + [(cut, BF16)] * len(pairs),
        [SMEM, diag, diag] + [block_of((1, SLOTS, SIZE, SIZE), p) for p in pairs],
        [block_of((BLOCK, SIZE)), block_of((NT, BLOCK, SIZE))] + [block_of(cut)] * len(pairs),
        (place, rhs, dinv) + (tiles,) * len(pairs),
        moved=2**22,
    )


def masked(block, alive):
    return jnp.where(alive, block, jnp.zeros_like(block))


def pick_kernel(pairs, place, here, there, known, *outs):
    mine = lax.rem(place[0], 2)
    for step in range(CHIPS):
        turn = (CHIPS - step) % CHIPS
        for core in range(2):
            for n, pair in enumerate(pairs):
                for slot in range(SLOTS):
                    at = jnp.where(mine == core, here[turn, slot, pair], there[turn, slot, pair])
                    outs[step][n, core * SLOTS + slot] = known[at]


def pick_call(name, pairs, place, here, there, known):
    shape = (len(pairs), 2 * SLOTS, BLOCK, SIZE)
    return call(
        functools.partial(pick_kernel, pairs),
        name,
        [(shape, BF16)] * CHIPS,
        [SMEM, SMEM, SMEM, block_of((NT, BLOCK, SIZE))],
        [block_of(shape)] * CHIPS,
        (place, here, there, known),
        moved=2**21,
    )


def partial_kernel(pairs, kept, place, live, *refs):
    refs = list(refs)
    got = [refs.pop(0) for _ in range(CHIPS)]
    before = [refs.pop(0) for _ in range(CHIPS)] if kept else []
    tiles = [(refs.pop(0), refs.pop(0)) for _ in pairs]
    chip, core = lax.div(place[0], 2), lax.rem(place[0], 2)
    for n, pair in enumerate(pairs):
        total = jnp.zeros((CHIPS * BLOCK, SIZE), F32)
        for swapped in range(2):
            side = lax.rem(core + swapped, 2)
            for slot in range(SLOTS):
                at = side * SLOTS + slot
                block = jnp.concatenate([g[n, at] for g in got])
                block = masked(block, chip * 2 * SLOTS + at < live[0, pair])
                total = total + dot_nt(block, tiles[n][swapped][0, slot])
        for step in range(CHIPS):
            sums = total[step * BLOCK : (step + 1) * BLOCK]
            refs[n * CHIPS + step][...] = sums + before[step][...] if kept else sums


def partial_call(name, pairs, place, live, got, kept, tiles, swapped):
    shape = (BLOCK, SIZE)
    args = [place, live, *got, *kept]
    specs = [SMEM, SMEM] + [block_of(g.shape) for g in args[2:]]
    for pair in pairs:
        args += [tiles, swapped]
        specs += [block_of((1, SLOTS, SIZE, SIZE), pair)] * 2
    return call(
        functools.partial(partial_kernel, pairs, bool(kept)),
        name,
        [(shape, F32)] * (CHIPS * len(pairs)),
        specs,
        [block_of(shape)] * (CHIPS * len(pairs)),
        args,
        flops=2 * 6 * SIZE**3,
        moved=2**21,
    )


def level_kernel(pair, count, returned, earlier, place, here, there, live, rhs, dinv, known, *refs):
    refs = list(refs)
    tiles = [refs.pop(0) for _ in range(count)]
    back = [refs.pop(0) for _ in range(returned)]
    before = [refs.pop(0) for _ in range(earlier)]
    held, sems = refs[-2:]
    chip, core = lax.div(place[0], 2), lax.rem(place[0], 2)
    chips = [lax.rem(chip + CHIPS - d, CHIPS) for d in range(CHIPS)]
    split = count == 2
    copies = [
        [pltpu.make_async_copy(tiles[n].at[chips[d]], held.at[2 * d + n], sems.at[2 * d + n]) for n in range(2)]
        if split
        else [pltpu.make_async_copy(tiles[0].at[pl.ds(2 * chips[d], 2)], held.at[pl.ds(2 * d, 2)], sems.at[2 * d])]
        for d in range(CHIPS)
    ]
    for copy in sum(copies, []):
        copy.start()
    total = probe_rows(place[0], rhs[0])
    for sums in back:
        total = total - sums[...]
    for d in range(CHIPS):
        for copy in copies[d]:
            copy.wait()
        for n, (cols, side) in enumerate(((here, core), (there, 1 - core))):
            first = (2 * chips[d] + side) * SLOTS
            at = 2 * d + (n if split else side)
            for slot in range(SLOTS):
                block = masked(known[cols[d, slot, pair]], first + slot < live[0, pair])
                total = total - dot_nt(block, held[at, slot * SIZE : (slot + 1) * SIZE])
    result = dot_nt(total.astype(BF16), dinv[0])
    if earlier:
        for n in range(earlier):
            refs[0][n] = before[n][...]
        refs[0][earlier] = result
        return
    refs[0][...] = result
    spread_out(result, refs[1])


def level_call(level, pair, place, here, there, live, rhs, dinv, known, tiles, back, earlier):
    flat, pick = block_of((BLOCK, SIZE)), block_of((1, SIZE, SIZE), level)
    if earlier:
        shapes, outs = [((level + 1, BLOCK, SIZE), F32)], [block_of((level + 1, BLOCK, SIZE))]
    else:
        shapes = [((BLOCK, SIZE), F32), ((NT, BLOCK, SIZE), BF16)]
        outs = [flat, block_of((NT, BLOCK, SIZE))]
    return call(
        functools.partial(level_kernel, pair, len(tiles), len(back), len(earlier)),
        "level%d" % level,
        shapes,
        [SMEM] * 4 + [pick, pick, block_of((NT, BLOCK, SIZE))] + [ANY] * len(tiles) + [flat] * (len(back) + len(earlier)),
        outs,
        (place, here, there, live, rhs, dinv, known, *tiles, *back, *earlier),
        [pltpu.VMEM((PLACES, SLOTS * SIZE, SIZE), BF16), pltpu.SemaphoreType.DMA((PLACES,))],
        flops=2 * 24 * BLOCK * SIZE * SIZE,
        moved=24 * SIZE * SIZE * 2,
    )


def local(rhs, dinv, factor, cols, live):
    place = lax.axis_index(COL).astype(jnp.int32).reshape(1)
    tiles = factor.transpose(0, 2, 1, 3)
    move = lambda array, pairs: lax.ppermute(array, COL, pairs)
    over_row = lambda array: lax.all_to_all(array, "row", 0, 0, tiled=True)

    gather = lambda array, axes: lax.all_gather(array, axes, axis=0, tiled=False)
    live = live.transpose(1, 0)

    own = cols.transpose(2, 1, 0).reshape(SLOTS, -1)
    here = jnp.stack([own] + [move(own, TURN[d]) for d in range(1, CHIPS)])
    there = move(here, SWAP)
    answer0, spread0, *cuts = first_call(place, rhs, dinv, tiles, (0, 2, 5))
    gathered0, gathered2, gathered5 = gather(cuts[0], "chip"), gather(cuts[1], COL), gather(cuts[2], COL)

    def send(picked):
        return [picked[0]] + [move(picked[d], TURN[d]) for d in range(1, CHIPS)]

    def give_back(sums):
        return [sums[0]] + [move(sums[d], TURN[CHIPS - d]) for d in range(1, CHIPS)]

    later, spread0 = lax.optimization_barrier((tiles, spread0))
    swapped = move(later, SWAP)
    known0 = over_row(spread0)
    picked = pick_call("pick13", (1, 3), place, here, there, known0)
    known0, *picked = lax.optimization_barrier((known0, *picked))
    got = send(picked)
    gathered0, _ = lax.optimization_barrier((gathered0, picked[0]))
    gathered0 = [gathered0, move(gathered0, SWAP)]
    answer1, spread1 = level_call(1, 0, place, here, there, live, rhs, dinv, known0, gathered0, [], [])
    spread1, *got = lax.optimization_barrier((spread1, *got))
    known1 = over_row(spread1)

    sums = partial_call("partial13", (1, 3), place, live, got, [], tiles, swapped)
    sums2, sums3 = sums[:CHIPS], sums[CHIPS:]
    back2 = give_back(sums2)
    known1, *back2 = lax.optimization_barrier((known1, *back2))
    picked = pick_call("pick4", (4,), place, here, there, known1)
    known1, *picked = lax.optimization_barrier((known1, *picked))
    got = send(picked)
    answer2, spread2 = level_call(2, 2, place, here, there, live, rhs, dinv, known1, [gathered2], back2, [])
    spread2, *got = lax.optimization_barrier((spread2, *got))
    known2 = over_row(spread2)

    sums3 = partial_call("partial4", (4,), place, live, got, sums3, tiles, swapped)
    (solved,) = level_call(
        3, 5, place, here, there, live, rhs, dinv, known2, [gathered5], give_back(sums3), [answer0, answer1, answer2]
    )
    return solved.transpose(0, 2, 1)


def solution(mesh):
    rows, places = mesh.devices.shape
    mesh = jax.sharding.Mesh(mesh.devices.reshape(rows, places // 2, 2), ("row",) + COL)
    in_specs = (
        P(None, "row", None),
        P(None, "row", None),
        P(None, "row", COL, None),
        P(None, "row", COL),
        P(None, "row"),
    )
    out_specs = P(None, "row", COL)
    return jax.shard_map(local, mesh=mesh, in_specs=in_specs, out_specs=out_specs, check_vma=False)
```

```python
import functools

import jax
import jax.numpy as jnp
from jax import lax
from jax.experimental import pallas as pl
from jax.experimental.pallas import tpu as pltpu
from jax.sharding import PartitionSpec as P

NT_DIMS = (((1,), (1,)), ((), ()))
BLOCK = 32
SIZE = 256
SLOTS = 3
PLACES = 8
CHIPS = 4
NT = 32
VMEM_BYTES = 64 * 1024 * 1024
SMEM = pl.BlockSpec(memory_space=pltpu.SMEM)
ANY = pl.BlockSpec(memory_space=pl.ANY)
F32, BF16 = jnp.float32, jnp.bfloat16
COL = ("chip", "core")
SWAP = [(p, p ^ 1) for p in range(PLACES)]
TURN = [[(p, (p + 2 * d) % PLACES) for p in range(PLACES)] for d in range(CHIPS)]


def dot_nt(a, b):
    return lax.dot_general(a, b, NT_DIMS, preferred_element_type=F32)


def block_of(shape, *lead):
    return pl.BlockSpec(shape, lambda i: tuple(lead) + (0,) * (len(shape) - len(lead)))


def probe_rows(place, rhs):
    probe = lax.broadcasted_iota(jnp.int32, (BLOCK, rhs.shape[1]), 1)
    mine = lax.broadcasted_iota(jnp.int32, (BLOCK, rhs.shape[1]), 0) + place * BLOCK
    return dot_nt((probe == mine).astype(BF16), rhs)


def spread_out(result, spread):
    rounded = result.astype(BF16)
    for copy in range(spread.shape[0]):
        spread[copy] = rounded


def call(kernel, name, shapes, in_specs, out_specs, args, scratch=(), flops=0, moved=0):
    return pl.pallas_call(
        kernel,
        grid=(1,),
        out_shape=tuple(jax.ShapeDtypeStruct(s, t) for s, t in shapes),
        in_specs=in_specs,
        out_specs=tuple(out_specs),
        scratch_shapes=list(scratch),
        cost_estimate=pl.CostEstimate(flops=flops, bytes_accessed=moved, transcendentals=0),
        compiler_params=pltpu.CompilerParams(vmem_limit_bytes=VMEM_BYTES),
        name=name,
    )(*args)


def first_kernel(place, rhs, dinv, *refs):
    count = (len(refs) - 2) // 2
    tiles, (answer, spread), cuts = refs[:count], refs[count : count + 2], refs[count + 2 :]
    residual = probe_rows(place[0], rhs[0]).astype(BF16)
    result = dot_nt(residual, dinv[0])
    answer[...] = result
    spread_out(result, spread)
    for n in range(count):
        for slot in range(SLOTS):
            cuts[n][slot * SIZE : (slot + 1) * SIZE] = tiles[n][0, slot]


def first_call(place, rhs, dinv, tiles, pairs):
    diag, cut = block_of((1, SIZE, SIZE), 0), (SLOTS * SIZE, SIZE)
    return call(
        first_kernel,
        "level0",
        [((BLOCK, SIZE), F32), ((NT, BLOCK, SIZE), BF16)] + [(cut, BF16)] * len(pairs),
        [SMEM, diag, diag] + [block_of((1, SLOTS, SIZE, SIZE), p) for p in pairs],
        [block_of((BLOCK, SIZE)), block_of((NT, BLOCK, SIZE))] + [block_of(cut)] * len(pairs),
        (place, rhs, dinv) + (tiles,) * len(pairs),
        moved=2**22,
    )


def masked(block, alive):
    return jnp.where(alive, block, jnp.zeros_like(block))


def pick_kernel(pairs, place, here, there, known, *outs):
    mine = lax.rem(place[0], 2)
    for step in range(CHIPS):
        turn = (CHIPS - step) % CHIPS
        for core in range(2):
            for n, pair in enumerate(pairs):
                for slot in range(SLOTS):
                    at = jnp.where(mine == core, here[turn, slot, pair], there[turn, slot, pair])
                    outs[step][n, core * SLOTS + slot] = known[at]


def pick_call(name, pairs, place, here, there, known):
    shape = (len(pairs), 2 * SLOTS, BLOCK, SIZE)
    return call(
        functools.partial(pick_kernel, pairs),
        name,
        [(shape, BF16)] * CHIPS,
        [SMEM, SMEM, SMEM, block_of((NT, BLOCK, SIZE))],
        [block_of(shape)] * CHIPS,
        (place, here, there, known),
        moved=2**21,
    )


def partial_kernel(pairs, kept, place, live, *refs):
    refs = list(refs)
    got = [refs.pop(0) for _ in range(CHIPS)]
    before = [refs.pop(0) for _ in range(CHIPS)] if kept else []
    tiles = [(refs.pop(0), refs.pop(0)) for _ in pairs]
    chip, core = lax.div(place[0], 2), lax.rem(place[0], 2)
    for n, pair in enumerate(pairs):
        total = jnp.zeros((CHIPS * BLOCK, SIZE), F32)
        for swapped in range(2):
            side = lax.rem(core + swapped, 2)
            for slot in range(SLOTS):
                at = side * SLOTS + slot
                block = jnp.concatenate([g[n, at] for g in got])
                block = masked(block, chip * 2 * SLOTS + at < live[0, pair])
                total = total + dot_nt(block, tiles[n][swapped][0, slot])
        for step in range(CHIPS):
            sums = total[step * BLOCK : (step + 1) * BLOCK]
            refs[n * CHIPS + step][...] = sums + before[step][...] if kept else sums


def partial_call(name, pairs, place, live, got, kept, tiles, swapped):
    shape = (BLOCK, SIZE)
    args = [place, live, *got, *kept]
    specs = [SMEM, SMEM] + [block_of(g.shape) for g in args[2:]]
    for pair in pairs:
        args += [tiles, swapped]
        specs += [block_of((1, SLOTS, SIZE, SIZE), pair)] * 2
    return call(
        functools.partial(partial_kernel, pairs, bool(kept)),
        name,
        [(shape, F32)] * (CHIPS * len(pairs)),
        specs,
        [block_of(shape)] * (CHIPS * len(pairs)),
        args,
        flops=2 * 6 * SIZE**3,
        moved=2**21,
    )


def level_kernel(pair, count, returned, earlier, place, here, there, live, rhs, dinv, known, *refs):
    refs = list(refs)
    tiles = [refs.pop(0) for _ in range(count)]
    back = [refs.pop(0) for _ in range(returned)]
    before = [refs.pop(0) for _ in range(earlier)]
    held, sems = refs[-2:]
    chip, core = lax.div(place[0], 2), lax.rem(place[0], 2)
    chips = [lax.rem(chip + CHIPS - d, CHIPS) for d in range(CHIPS)]
    split = count == 2
    copies = [
        [pltpu.make_async_copy(tiles[n].at[chips[d]], held.at[2 * d + n], sems.at[2 * d + n]) for n in range(2)]
        if split
        else [pltpu.make_async_copy(tiles[0].at[pl.ds(2 * chips[d], 2)], held.at[pl.ds(2 * d, 2)], sems.at[2 * d])]
        for d in range(CHIPS)
    ]
    for copy in sum(copies, []):
        copy.start()
    total = probe_rows(place[0], rhs[0])
    for sums in back:
        total = total - sums[...]
    for d in range(CHIPS):
        for copy in copies[d]:
            copy.wait()
        for n, (cols, side) in enumerate(((here, core), (there, 1 - core))):
            first = (2 * chips[d] + side) * SLOTS
            at = 2 * d + (n if split else side)
            for slot in range(SLOTS):
                block = masked(known[cols[d, slot, pair]], first + slot < live[0, pair])
                total = total - dot_nt(block, held[at, slot * SIZE : (slot + 1) * SIZE])
    result = dot_nt(total.astype(BF16), dinv[0])
    if earlier:
        for n in range(earlier):
            refs[0][n] = before[n][...]
        refs[0][earlier] = result
        return
    refs[0][...] = result
    spread_out(result, refs[1])


def level_call(level, pair, place, here, there, live, rhs, dinv, known, tiles, back, earlier):
    flat, pick = block_of((BLOCK, SIZE)), block_of((1, SIZE, SIZE), level)
    if earlier:
        shapes, outs = [((level + 1, BLOCK, SIZE), F32)], [block_of((level + 1, BLOCK, SIZE))]
    else:
        shapes = [((BLOCK, SIZE), F32), ((NT, BLOCK, SIZE), BF16)]
        outs = [flat, block_of((NT, BLOCK, SIZE))]
    return call(
        functools.partial(level_kernel, pair, len(tiles), len(back), len(earlier)),
        "level%d" % level,
        shapes,
        [SMEM] * 4 + [pick, pick, block_of((NT, BLOCK, SIZE))] + [ANY] * len(tiles) + [flat] * (len(back) + len(earlier)),
        outs,
        (place, here, there, live, rhs, dinv, known, *tiles, *back, *earlier),
        [pltpu.VMEM((PLACES, SLOTS * SIZE, SIZE), BF16), pltpu.SemaphoreType.DMA((PLACES,))],
        flops=2 * 24 * BLOCK * SIZE * SIZE,
        moved=24 * SIZE * SIZE * 2,
    )


def local(rhs, dinv, factor, cols, live):
    place = lax.axis_index(COL).astype(jnp.int32).reshape(1)
    tiles = factor.transpose(0, 2, 1, 3)
    move = lambda array, pairs: lax.ppermute(array, COL, pairs)
    over_row = lambda array: lax.all_to_all(array, "row", 0, 0, tiled=True)

    gather = lambda array, axes: lax.all_gather(array, axes, axis=0, tiled=False)
    live = live.transpose(1, 0)

    own = cols.transpose(2, 1, 0).reshape(SLOTS, -1)
    here = jnp.stack([own] + [move(own, TURN[d]) for d in range(1, CHIPS)])
    there = move(here, SWAP)
    answer0, spread0, *cuts = first_call(place, rhs, dinv, tiles, (0, 2, 5))
    gathered0, gathered2, gathered5 = gather(cuts[0], COL), gather(cuts[1], "chip"), gather(cuts[2], COL)

    def send(picked):
        return [picked[0]] + [move(picked[d], TURN[d]) for d in range(1, CHIPS)]

    def give_back(sums):
        return [sums[0]] + [move(sums[d], TURN[CHIPS - d]) for d in range(1, CHIPS)]

    known0 = over_row(spread0)
    picked = pick_call("pick13", (1, 3), place, here, there, known0)
    later, known0, *picked = lax.optimization_barrier((tiles, known0, *picked))
    swapped = move(later, SWAP)
    got = send(picked)
    answer1, spread1 = level_call(1, 0, place, here, there, live, rhs, dinv, known0, [gathered0], [], [])
    spread1, *got = lax.optimization_barrier((spread1, *got))
    known1 = over_row(spread1)

    sums = partial_call("partial13", (1, 3), place, live, got, [], tiles, swapped)
    sums2, sums3 = sums[:CHIPS], sums[CHIPS:]
    back2 = give_back(sums2)
    known1, *back2 = lax.optimization_barrier((known1, *back2))
    picked = pick_call("pick4", (4,), place, here, there, known1)
    known1, *picked = lax.optimization_barrier((known1, *picked))
    got = send(picked)
    gathered2, _ = lax.optimization_barrier((gathered2, picked[0]))
    gathered2 = [gathered2, move(gathered2, SWAP)]
    answer2, spread2 = level_call(2, 2, place, here, there, live, rhs, dinv, known1, gathered2, back2, [])
    spread2, *got = lax.optimization_barrier((spread2, *got))
    known2 = over_row(spread2)

    sums3 = partial_call("partial4", (4,), place, live, got, sums3, tiles, swapped)
    (solved,) = level_call(
        3, 5, place, here, there, live, rhs, dinv, known2, [gathered5], give_back(sums3), [answer0, answer1, answer2]
    )
    return solved.transpose(0, 2, 1)


def solution(mesh):
    rows, places = mesh.devices.shape
    mesh = jax.sharding.Mesh(mesh.devices.reshape(rows, places // 2, 2), ("row",) + COL)
    in_specs = (
        P(None, "row", None),
        P(None, "row", None),
        P(None, "row", COL, None),
        P(None, "row", COL),
        P(None, "row"),
    )
    out_specs = P(None, "row", COL)
    return jax.shard_map(local, mesh=mesh, in_specs=in_specs, out_specs=out_specs, check_vma=False)
```

```python
import functools

import jax
import jax.numpy as jnp
from jax import lax
from jax.experimental import pallas as pl
from jax.experimental.pallas import tpu as pltpu
from jax.sharding import PartitionSpec as P

NT_DIMS = (((1,), (1,)), ((), ()))
BLOCK = 32
SIZE = 256
SLOTS = 3
PLACES = 8
CHIPS = 4
NT = 32
VMEM_BYTES = 64 * 1024 * 1024
SMEM = pl.BlockSpec(memory_space=pltpu.SMEM)
ANY = pl.BlockSpec(memory_space=pl.ANY)
F32, BF16 = jnp.float32, jnp.bfloat16
COL = ("chip", "core")
SWAP = [(p, p ^ 1) for p in range(PLACES)]
TURN = [[(p, (p + 2 * d) % PLACES) for p in range(PLACES)] for d in range(CHIPS)]


def dot_nt(a, b):
    return lax.dot_general(a, b, NT_DIMS, preferred_element_type=F32)


def block_of(shape, *lead):
    return pl.BlockSpec(shape, lambda i: tuple(lead) + (0,) * (len(shape) - len(lead)))


def probe_rows(place, rhs):
    probe = lax.broadcasted_iota(jnp.int32, (BLOCK, rhs.shape[1]), 1)
    mine = lax.broadcasted_iota(jnp.int32, (BLOCK, rhs.shape[1]), 0) + place * BLOCK
    return dot_nt((probe == mine).astype(BF16), rhs)


def spread_out(result, spread):
    rounded = result.astype(BF16)
    for copy in range(spread.shape[0]):
        spread[copy] = rounded


def call(kernel, name, shapes, in_specs, out_specs, args, scratch=(), flops=0, moved=0):
    return pl.pallas_call(
        kernel,
        grid=(1,),
        out_shape=tuple(jax.ShapeDtypeStruct(s, t) for s, t in shapes),
        in_specs=in_specs,
        out_specs=tuple(out_specs),
        scratch_shapes=list(scratch),
        cost_estimate=pl.CostEstimate(flops=flops, bytes_accessed=moved, transcendentals=0),
        compiler_params=pltpu.CompilerParams(vmem_limit_bytes=VMEM_BYTES),
        name=name,
    )(*args)


def cut_kernel(tiles, cut):
    for slot in range(SLOTS):
        cut[slot * SIZE : (slot + 1) * SIZE] = tiles[0, slot]


def cut_call(tiles, pair):
    cut = (SLOTS * SIZE, SIZE)
    return call(
        cut_kernel,
        "cut",
        [(cut, BF16)],
        [block_of((1, SLOTS, SIZE, SIZE), pair)],
        [block_of(cut)],
        (tiles,),
        moved=2**20,
    )[0]


def first_kernel(place, rhs, dinv, *refs):
    count = (len(refs) - 2) // 2
    tiles, (answer, spread), cuts = refs[:count], refs[count : count + 2], refs[count + 2 :]
    residual = probe_rows(place[0], rhs[0]).astype(BF16)
    result = dot_nt(residual, dinv[0])
    answer[...] = result
    spread_out(result, spread)
    for n in range(count):
        for slot in range(SLOTS):
            cuts[n][slot * SIZE : (slot + 1) * SIZE] = tiles[n][0, slot]


def first_call(place, rhs, dinv, tiles, pairs):
    diag, cut = block_of((1, SIZE, SIZE), 0), (SLOTS * SIZE, SIZE)
    return call(
        first_kernel,
        "level0",
        [((BLOCK, SIZE), F32), ((NT, BLOCK, SIZE), BF16)] + [(cut, BF16)] * len(pairs),
        [SMEM, diag, diag] + [block_of((1, SLOTS, SIZE, SIZE), p) for p in pairs],
        [block_of((BLOCK, SIZE)), block_of((NT, BLOCK, SIZE))] + [block_of(cut)] * len(pairs),
        (place, rhs, dinv) + (tiles,) * len(pairs),
        moved=2**22,
    )


def masked(block, alive):
    return jnp.where(alive, block, jnp.zeros_like(block))


def pick_kernel(pairs, place, here, there, known, *outs):
    mine = lax.rem(place[0], 2)
    for step in range(CHIPS):
        turn = (CHIPS - step) % CHIPS
        for core in range(2):
            for n, pair in enumerate(pairs):
                for slot in range(SLOTS):
                    at = jnp.where(mine == core, here[turn, slot, pair], there[turn, slot, pair])
                    outs[step][n, core * SLOTS + slot] = known[at]


def pick_call(name, pairs, place, here, there, known):
    shape = (len(pairs), 2 * SLOTS, BLOCK, SIZE)
    return call(
        functools.partial(pick_kernel, pairs),
        name,
        [(shape, BF16)] * CHIPS,
        [SMEM, SMEM, SMEM, block_of((NT, BLOCK, SIZE))],
        [block_of(shape)] * CHIPS,
        (place, here, there, known),
        moved=2**21,
    )


def partial_kernel(pairs, kept, place, live, *refs):
    refs = list(refs)
    got = [refs.pop(0) for _ in range(CHIPS)]
    before = [refs.pop(0) for _ in range(CHIPS)] if kept else []
    tiles = [(refs.pop(0), refs.pop(0)) for _ in pairs]
    chip, core = lax.div(place[0], 2), lax.rem(place[0], 2)
    for n, pair in enumerate(pairs):
        total = jnp.zeros((CHIPS * BLOCK, SIZE), F32)
        for swapped in range(2):
            side = lax.rem(core + swapped, 2)
            for slot in range(SLOTS):
                at = side * SLOTS + slot
                block = jnp.concatenate([g[n, at] for g in got])
                block = masked(block, chip * 2 * SLOTS + at < live[0, pair])
                total = total + dot_nt(block, tiles[n][swapped][0, slot])
        for step in range(CHIPS):
            sums = total[step * BLOCK : (step + 1) * BLOCK]
            refs[n * CHIPS + step][...] = sums + before[step][...] if kept else sums


def partial_call(name, pairs, place, live, got, kept, tiles, swapped):
    shape = (BLOCK, SIZE)
    args = [place, live, *got, *kept]
    specs = [SMEM, SMEM] + [block_of(g.shape) for g in args[2:]]
    for pair in pairs:
        args += [tiles, swapped]
        specs += [block_of((1, SLOTS, SIZE, SIZE), pair)] * 2
    return call(
        functools.partial(partial_kernel, pairs, bool(kept)),
        name,
        [(shape, F32)] * (CHIPS * len(pairs)),
        specs,
        [block_of(shape)] * (CHIPS * len(pairs)),
        args,
        flops=2 * 6 * SIZE**3,
        moved=2**21,
    )


def level_kernel(pair, count, returned, earlier, place, here, there, live, rhs, dinv, known, *refs):
    refs = list(refs)
    tiles = [refs.pop(0) for _ in range(count)]
    back = [refs.pop(0) for _ in range(returned)]
    before = [refs.pop(0) for _ in range(earlier)]
    held, sems = refs[-2:]
    chip, core = lax.div(place[0], 2), lax.rem(place[0], 2)
    chips = [lax.rem(chip + CHIPS - d, CHIPS) for d in range(CHIPS)]
    split = count == 2
    copies = [
        [pltpu.make_async_copy(tiles[n].at[chips[d]], held.at[2 * d + n], sems.at[2 * d + n]) for n in range(2)]
        if split
        else [pltpu.make_async_copy(tiles[0].at[pl.ds(2 * chips[d], 2)], held.at[pl.ds(2 * d, 2)], sems.at[2 * d])]
        for d in range(CHIPS)
    ]
    for copy in sum(copies, []):
        copy.start()
    total = probe_rows(place[0], rhs[0])
    for sums in back:
        total = total - sums[...]
    for d in range(CHIPS):
        for copy in copies[d]:
            copy.wait()
        for n, (cols, side) in enumerate(((here, core), (there, 1 - core))):
            first = (2 * chips[d] + side) * SLOTS
            at = 2 * d + (n if split else side)
            for slot in range(SLOTS):
                block = masked(known[cols[d, slot, pair]], first + slot < live[0, pair])
                total = total - dot_nt(block, held[at, slot * SIZE : (slot + 1) * SIZE])
    result = dot_nt(total.astype(BF16), dinv[0])
    if earlier:
        for n in range(earlier):
            refs[0][n] = before[n][...]
        refs[0][earlier] = result
        return
    refs[0][...] = result
    spread_out(result, refs[1])


def level_call(level, pair, place, here, there, live, rhs, dinv, known, tiles, back, earlier):
    flat, pick = block_of((BLOCK, SIZE)), block_of((1, SIZE, SIZE), level)
    if earlier:
        shapes, outs = [((level + 1, BLOCK, SIZE), F32)], [block_of((level + 1, BLOCK, SIZE))]
    else:
        shapes = [((BLOCK, SIZE), F32), ((NT, BLOCK, SIZE), BF16)]
        outs = [flat, block_of((NT, BLOCK, SIZE))]
    return call(
        functools.partial(level_kernel, pair, len(tiles), len(back), len(earlier)),
        "level%d" % level,
        shapes,
        [SMEM] * 4 + [pick, pick, block_of((NT, BLOCK, SIZE))] + [ANY] * len(tiles) + [flat] * (len(back) + len(earlier)),
        outs,
        (place, here, there, live, rhs, dinv, known, *tiles, *back, *earlier),
        [pltpu.VMEM((PLACES, SLOTS * SIZE, SIZE), BF16), pltpu.SemaphoreType.DMA((PLACES,))],
        flops=2 * 24 * BLOCK * SIZE * SIZE,
        moved=24 * SIZE * SIZE * 2,
    )


def local(rhs, dinv, factor, cols, live):
    place = lax.axis_index(COL).astype(jnp.int32).reshape(1)
    tiles = factor.transpose(0, 2, 1, 3)
    move = lambda array, pairs: lax.ppermute(array, COL, pairs)
    over_row = lambda array: lax.all_to_all(array, "row", 0, 0, tiled=True)

    gather = lambda array, axes: lax.all_gather(array, axes, axis=0, tiled=False)
    live = live.transpose(1, 0)

    own = cols.transpose(2, 1, 0).reshape(SLOTS, -1)
    here = jnp.stack([own] + [move(own, TURN[d]) for d in range(1, CHIPS)])
    there = move(here, SWAP)
    cut0 = cut_call(tiles, 0)
    gathered0 = gather(cut0, COL)
    early, cut0 = lax.optimization_barrier((rhs, cut0))
    answer0, spread0, cut2, cut5 = first_call(place, early, dinv, tiles, (2, 5))
    gathered2, gathered5 = gather(cut2, "chip"), gather(cut5, COL)

    def send(picked):
        return [picked[0]] + [move(picked[d], TURN[d]) for d in range(1, CHIPS)]

    def give_back(sums):
        return [sums[0]] + [move(sums[d], TURN[CHIPS - d]) for d in range(1, CHIPS)]

    known0 = over_row(spread0)
    picked = pick_call("pick13", (1, 3), place, here, there, known0)
    later, known0, *picked = lax.optimization_barrier((tiles, known0, *picked))
    swapped = move(later, SWAP)
    got = send(picked)
    answer1, spread1 = level_call(1, 0, place, here, there, live, rhs, dinv, known0, [gathered0], [], [])
    spread1, *got = lax.optimization_barrier((spread1, *got))
    known1 = over_row(spread1)

    sums = partial_call("partial13", (1, 3), place, live, got, [], tiles, swapped)
    sums2, sums3 = sums[:CHIPS], sums[CHIPS:]
    back2 = give_back(sums2)
    known1, *back2 = lax.optimization_barrier((known1, *back2))
    picked = pick_call("pick4", (4,), place, here, there, known1)
    known1, *picked = lax.optimization_barrier((known1, *picked))
    got = send(picked)
    gathered2, _ = lax.optimization_barrier((gathered2, picked[0]))
    gathered2 = [gathered2, move(gathered2, SWAP)]
    answer2, spread2 = level_call(2, 2, place, here, there, live, rhs, dinv, known1, gathered2, back2, [])
    spread2, *got = lax.optimization_barrier((spread2, *got))
    known2 = over_row(spread2)

    sums3 = partial_call("partial4", (4,), place, live, got, sums3, tiles, swapped)
    (solved,) = level_call(
        3, 5, place, here, there, live, rhs, dinv, known2, [gathered5], give_back(sums3), [answer0, answer1, answer2]
    )
    return solved.transpose(0, 2, 1)


def solution(mesh):
    rows, places = mesh.devices.shape
    mesh = jax.sharding.Mesh(mesh.devices.reshape(rows, places // 2, 2), ("row",) + COL)
    in_specs = (
        P(None, "row", None),
        P(None, "row", None),
        P(None, "row", COL, None),
        P(None, "row", COL),
        P(None, "row"),
    )
    out_specs = P(None, "row", COL)
    return jax.shard_map(local, mesh=mesh, in_specs=in_specs, out_specs=out_specs, check_vma=False)
```

```python
import functools

import jax
import jax.numpy as jnp
from jax import lax
from jax.experimental import pallas as pl
from jax.experimental.pallas import tpu as pltpu
from jax.sharding import PartitionSpec as P

NT_DIMS = (((1,), (1,)), ((), ()))
BLOCK = 32
SIZE = 256
SLOTS = 3
PLACES = 8
CHIPS = 4
NT = 32
VMEM_BYTES = 64 * 1024 * 1024
SMEM = pl.BlockSpec(memory_space=pltpu.SMEM)
ANY = pl.BlockSpec(memory_space=pl.ANY)
F32, BF16 = jnp.float32, jnp.bfloat16
COL = ("chip", "core")
SWAP = [(p, p ^ 1) for p in range(PLACES)]
TURN = [[(p, (p + 2 * d) % PLACES) for p in range(PLACES)] for d in range(CHIPS)]


def dot_nt(a, b):
    return lax.dot_general(a, b, NT_DIMS, preferred_element_type=F32)


def block_of(shape, *lead):
    return pl.BlockSpec(shape, lambda i: tuple(lead) + (0,) * (len(shape) - len(lead)))


def probe_rows(place, rhs):
    probe = lax.broadcasted_iota(jnp.int32, (BLOCK, rhs.shape[1]), 1)
    mine = lax.broadcasted_iota(jnp.int32, (BLOCK, rhs.shape[1]), 0) + place * BLOCK
    return dot_nt((probe == mine).astype(BF16), rhs)


def spread_out(result, spread):
    rounded = result.astype(BF16)
    for copy in range(spread.shape[0]):
        spread[copy] = rounded


def call(kernel, name, shapes, in_specs, out_specs, args, scratch=(), flops=0, moved=0):
    return pl.pallas_call(
        kernel,
        grid=(1,),
        out_shape=tuple(jax.ShapeDtypeStruct(s, t) for s, t in shapes),
        in_specs=in_specs,
        out_specs=tuple(out_specs),
        scratch_shapes=list(scratch),
        cost_estimate=pl.CostEstimate(flops=flops, bytes_accessed=moved, transcendentals=0),
        compiler_params=pltpu.CompilerParams(vmem_limit_bytes=VMEM_BYTES),
        name=name,
    )(*args)


def first_kernel(place, rhs, dinv, *refs):
    count = (len(refs) - 2) // 2
    tiles, (answer, spread), cuts = refs[:count], refs[count : count + 2], refs[count + 2 :]
    residual = probe_rows(place[0], rhs[0]).astype(BF16)
    result = dot_nt(residual, dinv[0])
    answer[...] = result
    spread_out(result, spread)
    for n in range(count):
        for slot in range(SLOTS):
            cuts[n][slot * SIZE : (slot + 1) * SIZE] = tiles[n][0, slot]


def first_call(place, rhs, dinv, tiles, pairs):
    diag, cut = block_of((1, SIZE, SIZE), 0), (SLOTS * SIZE, SIZE)
    return call(
        first_kernel,
        "level0",
        [((BLOCK, SIZE), F32), ((NT, BLOCK, SIZE), BF16)] + [(cut, BF16)] * len(pairs),
        [SMEM, diag, diag] + [block_of((1, SLOTS, SIZE, SIZE), p) for p in pairs],
        [block_of((BLOCK, SIZE)), block_of((NT, BLOCK, SIZE))] + [block_of(cut)] * len(pairs),
        (place, rhs, dinv) + (tiles,) * len(pairs),
        moved=2**22,
    )


def masked(block, alive):
    return jnp.where(alive, block, jnp.zeros_like(block))


def pick_kernel(pairs, place, here, there, known, *outs):
    mine = lax.rem(place[0], 2)
    for step in range(CHIPS):
        turn = (CHIPS - step) % CHIPS
        for core in range(2):
            for n, pair in enumerate(pairs):
                for slot in range(SLOTS):
                    at = jnp.where(mine == core, here[turn, slot, pair], there[turn, slot, pair])
                    outs[step][n, core * SLOTS + slot] = known[at]


def pick_call(name, pairs, place, here, there, known):
    shape = (len(pairs), 2 * SLOTS, BLOCK, SIZE)
    return call(
        functools.partial(pick_kernel, pairs),
        name,
        [(shape, BF16)] * CHIPS,
        [SMEM, SMEM, SMEM, block_of((NT, BLOCK, SIZE))],
        [block_of(shape)] * CHIPS,
        (place, here, there, known),
        moved=2**21,
    )


def partial_kernel(pairs, kept, place, live, *refs):
    refs = list(refs)
    got = [refs.pop(0) for _ in range(CHIPS)]
    before = [refs.pop(0) for _ in range(CHIPS)] if kept else []
    tiles = [(refs.pop(0), refs.pop(0)) for _ in pairs]
    chip, core = lax.div(place[0], 2), lax.rem(place[0], 2)
    for n, pair in enumerate(pairs):
        total = jnp.zeros((CHIPS * BLOCK, SIZE), F32)
        for swapped in range(2):
            side = lax.rem(core + swapped, 2)
            for slot in range(SLOTS):
                at = side * SLOTS + slot
                block = jnp.concatenate([g[n, at] for g in got])
                block = masked(block, chip * 2 * SLOTS + at < live[0, pair])
                total = total + dot_nt(block, tiles[n][swapped][0, slot])
        for step in range(CHIPS):
            sums = total[step * BLOCK : (step + 1) * BLOCK]
            refs[n * CHIPS + step][...] = sums + before[step][...] if kept else sums


def partial_call(name, pairs, place, live, got, kept, tiles, swapped):
    shape = (BLOCK, SIZE)
    args = [place, live, *got, *kept]
    specs = [SMEM, SMEM] + [block_of(g.shape) for g in args[2:]]
    for pair in pairs:
        args += [tiles, swapped]
        specs += [block_of((1, SLOTS, SIZE, SIZE), pair)] * 2
    return call(
        functools.partial(partial_kernel, pairs, bool(kept)),
        name,
        [(shape, F32)] * (CHIPS * len(pairs)),
        specs,
        [block_of(shape)] * (CHIPS * len(pairs)),
        args,
        flops=2 * 6 * SIZE**3,
        moved=2**21,
    )


def level_kernel(pair, count, returned, earlier, place, here, there, live, rhs, dinv, known, *refs):
    refs = list(refs)
    tiles = [refs.pop(0) for _ in range(count)]
    back = [refs.pop(0) for _ in range(returned)]
    before = [refs.pop(0) for _ in range(earlier)]
    held, sems = refs[-2:]
    chip, core = lax.div(place[0], 2), lax.rem(place[0], 2)
    chips = [lax.rem(chip + CHIPS - d, CHIPS) for d in range(CHIPS)]
    split = count == 2
    copies = [
        [pltpu.make_async_copy(tiles[n].at[chips[d]], held.at[2 * d + n], sems.at[2 * d + n]) for n in range(2)]
        if split
        else [pltpu.make_async_copy(tiles[0].at[pl.ds(2 * chips[d], 2)], held.at[pl.ds(2 * d, 2)], sems.at[2 * d])]
        for d in range(CHIPS)
    ]
    for copy in sum(copies, []):
        copy.start()
    total = probe_rows(place[0], rhs[0])
    for sums in back:
        total = total - sums[...]
    for d in range(CHIPS):
        for copy in copies[d]:
            copy.wait()
        for n, (cols, side) in enumerate(((here, core), (there, 1 - core))):
            first = (2 * chips[d] + side) * SLOTS
            at = 2 * d + (n if split else side)
            for slot in range(SLOTS):
                block = masked(known[cols[d, slot, pair]], first + slot < live[0, pair])
                total = total - dot_nt(block, held[at, slot * SIZE : (slot + 1) * SIZE])
    result = dot_nt(total.astype(BF16), dinv[0])
    if earlier:
        for n in range(earlier):
            refs[0][n] = before[n][...]
        refs[0][earlier] = result
        return
    refs[0][...] = result
    spread_out(result, refs[1])


def level_call(level, pair, place, here, there, live, rhs, dinv, known, tiles, back, earlier):
    flat, pick = block_of((BLOCK, SIZE)), block_of((1, SIZE, SIZE), level)
    if earlier:
        shapes, outs = [((level + 1, BLOCK, SIZE), F32)], [block_of((level + 1, BLOCK, SIZE))]
    else:
        shapes = [((BLOCK, SIZE), F32), ((NT, BLOCK, SIZE), BF16)]
        outs = [flat, block_of((NT, BLOCK, SIZE))]
    return call(
        functools.partial(level_kernel, pair, len(tiles), len(back), len(earlier)),
        "level%d" % level,
        shapes,
        [SMEM] * 4 + [pick, pick, block_of((NT, BLOCK, SIZE))] + [ANY] * len(tiles) + [flat] * (len(back) + len(earlier)),
        outs,
        (place, here, there, live, rhs, dinv, known, *tiles, *back, *earlier),
        [pltpu.VMEM((PLACES, SLOTS * SIZE, SIZE), BF16), pltpu.SemaphoreType.DMA((PLACES,))],
        flops=2 * 24 * BLOCK * SIZE * SIZE,
        moved=24 * SIZE * SIZE * 2,
    )


def local(rhs, dinv, factor, cols, live):
    place = lax.axis_index(COL).astype(jnp.int32).reshape(1)
    tiles = factor.transpose(0, 2, 1, 3)
    move = lambda array, pairs: lax.ppermute(array, COL, pairs)
    over_row = lambda array: lax.all_to_all(array, "row", 0, 0, tiled=True)

    gather = lambda array, axes: lax.all_gather(array, axes, axis=0, tiled=False)
    live = live.transpose(1, 0)

    own = cols.transpose(2, 1, 0).reshape(SLOTS, -1)
    here = jnp.stack([own] + [move(own, TURN[d]) for d in range(1, CHIPS)])
    there = move(here, SWAP)
    answer0, spread0, *cuts = first_call(place, rhs, dinv, tiles, (0, 2, 5))
    gathered0, gathered2, gathered5 = gather(cuts[0], "chip"), gather(cuts[1], "chip"), gather(cuts[2], COL)

    def send(picked):
        return [picked[0]] + [move(picked[d], TURN[d]) for d in range(1, CHIPS)]

    def give_back(sums):
        return [sums[0]] + [move(sums[d], TURN[CHIPS - d]) for d in range(1, CHIPS)]

    later, spread0 = lax.optimization_barrier((tiles, spread0))
    swapped = move(later, SWAP)
    known0 = over_row(spread0)
    picked = pick_call("pick13", (1, 3), place, here, there, known0)
    known0, *picked = lax.optimization_barrier((known0, *picked))
    got = send(picked)
    gathered0, _ = lax.optimization_barrier((gathered0, picked[0]))
    gathered0 = [gathered0, move(gathered0, SWAP)]
    answer1, spread1 = level_call(1, 0, place, here, there, live, rhs, dinv, known0, gathered0, [], [])
    spread1, *got = lax.optimization_barrier((spread1, *got))
    known1 = over_row(spread1)

    sums = partial_call("partial13", (1, 3), place, live, got, [], tiles, swapped)
    sums2, sums3 = sums[:CHIPS], sums[CHIPS:]
    back2 = give_back(sums2)
    known1, *back2 = lax.optimization_barrier((known1, *back2))
    picked = pick_call("pick4", (4,), place, here, there, known1)
    known1, *picked = lax.optimization_barrier((known1, *picked))
    got = send(picked)
    gathered2, _ = lax.optimization_barrier((gathered2, picked[0]))
    gathered2 = [gathered2, move(gathered2, SWAP)]
    answer2, spread2 = level_call(2, 2, place, here, there, live, rhs, dinv, known1, gathered2, back2, [])
    spread2, *got = lax.optimization_barrier((spread2, *got))
    known2 = over_row(spread2)

    sums3 = partial_call("partial4", (4,), place, live, got, sums3, tiles, swapped)
    (solved,) = level_call(
        3, 5, place, here, there, live, rhs, dinv, known2, [gathered5], give_back(sums3), [answer0, answer1, answer2]
    )
    return solved.transpose(0, 2, 1)


def solution(mesh):
    rows, places = mesh.devices.shape
    mesh = jax.sharding.Mesh(mesh.devices.reshape(rows, places // 2, 2), ("row",) + COL)
    in_specs = (
        P(None, "row", None),
        P(None, "row", None),
        P(None, "row", COL, None),
        P(None, "row", COL),
        P(None, "row"),
    )
    out_specs = P(None, "row", COL)
    return jax.shard_map(local, mesh=mesh, in_specs=in_specs, out_specs=out_specs, check_vma=False)
```

```python
import functools

import jax
import jax.numpy as jnp
from jax import lax
from jax.experimental import pallas as pl
from jax.experimental.pallas import tpu as pltpu
from jax.sharding import PartitionSpec as P

NT_DIMS = (((1,), (1,)), ((), ()))
BLOCK = 32
SIZE = 256
SLOTS = 3
PLACES = 8
CHIPS = 4
NT = 32
VMEM_BYTES = 64 * 1024 * 1024
SMEM = pl.BlockSpec(memory_space=pltpu.SMEM)
ANY = pl.BlockSpec(memory_space=pl.ANY)
F32, BF16 = jnp.float32, jnp.bfloat16
COL = ("chip", "core")
SWAP = [(p, p ^ 1) for p in range(PLACES)]
TURN = [[(p, (p + 2 * d) % PLACES) for p in range(PLACES)] for d in range(CHIPS)]


def dot_nt(a, b):
    return lax.dot_general(a, b, NT_DIMS, preferred_element_type=F32)


def block_of(shape, *lead):
    return pl.BlockSpec(shape, lambda i: tuple(lead) + (0,) * (len(shape) - len(lead)))


def probe_rows(place, rhs):
    probe = lax.broadcasted_iota(jnp.int32, (BLOCK, rhs.shape[1]), 1)
    mine = lax.broadcasted_iota(jnp.int32, (BLOCK, rhs.shape[1]), 0) + place * BLOCK
    return dot_nt((probe == mine).astype(BF16), rhs)


def spread_out(result, spread):
    rounded = result.astype(BF16)
    for copy in range(spread.shape[0]):
        spread[copy] = rounded


def call(kernel, name, shapes, in_specs, out_specs, args, scratch=(), flops=0, moved=0):
    return pl.pallas_call(
        kernel,
        grid=(1,),
        out_shape=tuple(jax.ShapeDtypeStruct(s, t) for s, t in shapes),
        in_specs=in_specs,
        out_specs=tuple(out_specs),
        scratch_shapes=list(scratch),
        cost_estimate=pl.CostEstimate(flops=flops, bytes_accessed=moved, transcendentals=0),
        compiler_params=pltpu.CompilerParams(vmem_limit_bytes=VMEM_BYTES),
        name=name,
    )(*args)


def cut_kernel(tiles, cut):
    for slot in range(SLOTS):
        cut[slot * SIZE : (slot + 1) * SIZE] = tiles[0, slot]


def cut_call(tiles, pair):
    cut = (SLOTS * SIZE, SIZE)
    return call(
        cut_kernel,
        "cut",
        [(cut, BF16)],
        [block_of((1, SLOTS, SIZE, SIZE), pair)],
        [block_of(cut)],
        (tiles,),
        moved=2**20,
    )[0]


def first_kernel(place, rhs, dinv, *refs):
    count = (len(refs) - 2) // 2
    tiles, (answer, spread), cuts = refs[:count], refs[count : count + 2], refs[count + 2 :]
    residual = probe_rows(place[0], rhs[0]).astype(BF16)
    result = dot_nt(residual, dinv[0])
    answer[...] = result
    spread_out(result, spread)
    for n in range(count):
        for slot in range(SLOTS):
            cuts[n][slot * SIZE : (slot + 1) * SIZE] = tiles[n][0, slot]


def first_call(place, rhs, dinv, tiles, pairs):
    diag, cut = block_of((1, SIZE, SIZE), 0), (SLOTS * SIZE, SIZE)
    return call(
        first_kernel,
        "level0",
        [((BLOCK, SIZE), F32), ((NT, BLOCK, SIZE), BF16)] + [(cut, BF16)] * len(pairs),
        [SMEM, diag, diag] + [block_of((1, SLOTS, SIZE, SIZE), p) for p in pairs],
        [block_of((BLOCK, SIZE)), block_of((NT, BLOCK, SIZE))] + [block_of(cut)] * len(pairs),
        (place, rhs, dinv) + (tiles,) * len(pairs),
        moved=2**22,
    )


def masked(block, alive):
    return jnp.where(alive, block, jnp.zeros_like(block))


def pick_kernel(pairs, place, here, there, known, *outs):
    mine = lax.rem(place[0], 2)
    for step in range(CHIPS):
        turn = (CHIPS - step) % CHIPS
        for core in range(2):
            for n, pair in enumerate(pairs):
                for slot in range(SLOTS):
                    at = jnp.where(mine == core, here[turn, slot, pair], there[turn, slot, pair])
                    outs[step][n, core * SLOTS + slot] = known[at]


def pick_call(name, pairs, place, here, there, known):
    shape = (len(pairs), 2 * SLOTS, BLOCK, SIZE)
    return call(
        functools.partial(pick_kernel, pairs),
        name,
        [(shape, BF16)] * CHIPS,
        [SMEM, SMEM, SMEM, block_of((NT, BLOCK, SIZE))],
        [block_of(shape)] * CHIPS,
        (place, here, there, known),
        moved=2**21,
    )


def partial_kernel(pairs, kept, place, live, *refs):
    refs = list(refs)
    got = [refs.pop(0) for _ in range(CHIPS)]
    before = [refs.pop(0) for _ in range(CHIPS)] if kept else []
    tiles = [(refs.pop(0), refs.pop(0)) for _ in pairs]
    chip, core = lax.div(place[0], 2), lax.rem(place[0], 2)
    for n, pair in enumerate(pairs):
        total = jnp.zeros((CHIPS * BLOCK, SIZE), F32)
        for swapped in range(2):
            side = lax.rem(core + swapped, 2)
            for slot in range(SLOTS):
                at = side * SLOTS + slot
                block = jnp.concatenate([g[n, at] for g in got])
                block = masked(block, chip * 2 * SLOTS + at < live[0, pair])
                total = total + dot_nt(block, tiles[n][swapped][0, slot])
        for step in range(CHIPS):
            sums = total[step * BLOCK : (step + 1) * BLOCK]
            refs[n * CHIPS + step][...] = sums + before[step][...] if kept else sums


def partial_call(name, pairs, place, live, got, kept, tiles, swapped):
    shape = (BLOCK, SIZE)
    args = [place, live, *got, *kept]
    specs = [SMEM, SMEM] + [block_of(g.shape) for g in args[2:]]
    for pair in pairs:
        args += [tiles, swapped]
        specs += [block_of((1, SLOTS, SIZE, SIZE), pair)] * 2
    return call(
        functools.partial(partial_kernel, pairs, bool(kept)),
        name,
        [(shape, F32)] * (CHIPS * len(pairs)),
        specs,
        [block_of(shape)] * (CHIPS * len(pairs)),
        args,
        flops=2 * 6 * SIZE**3,
        moved=2**21,
    )


def level_kernel(pair, count, returned, earlier, place, here, there, live, rhs, dinv, known, *refs):
    refs = list(refs)
    tiles = [refs.pop(0) for _ in range(count)]
    back = [refs.pop(0) for _ in range(returned)]
    before = [refs.pop(0) for _ in range(earlier)]
    held, sems = refs[-2:]
    chip, core = lax.div(place[0], 2), lax.rem(place[0], 2)
    chips = [lax.rem(chip + CHIPS - d, CHIPS) for d in range(CHIPS)]
    split = count == 2
    copies = [
        [pltpu.make_async_copy(tiles[n].at[chips[d]], held.at[2 * d + n], sems.at[2 * d + n]) for n in range(2)]
        if split
        else [pltpu.make_async_copy(tiles[0].at[pl.ds(2 * chips[d], 2)], held.at[pl.ds(2 * d, 2)], sems.at[2 * d])]
        for d in range(CHIPS)
    ]
    for copy in sum(copies, []):
        copy.start()
    total = probe_rows(place[0], rhs[0])
    for sums in back:
        total = total - sums[...]
    for d in range(CHIPS):
        for copy in copies[d]:
            copy.wait()
        for n, (cols, side) in enumerate(((here, core), (there, 1 - core))):
            first = (2 * chips[d] + side) * SLOTS
            at = 2 * d + (n if split else side)
            for slot in range(SLOTS):
                block = masked(known[cols[d, slot, pair]], first + slot < live[0, pair])
                total = total - dot_nt(block, held[at, slot * SIZE : (slot + 1) * SIZE])
    result = dot_nt(total.astype(BF16), dinv[0])
    if earlier:
        for n in range(earlier):
            refs[0][n] = before[n][...]
        refs[0][earlier] = result
        return
    refs[0][...] = result
    spread_out(result, refs[1])


def level_call(level, pair, place, here, there, live, rhs, dinv, known, tiles, back, earlier):
    flat, pick = block_of((BLOCK, SIZE)), block_of((1, SIZE, SIZE), level)
    if earlier:
        shapes, outs = [((level + 1, BLOCK, SIZE), F32)], [block_of((level + 1, BLOCK, SIZE))]
    else:
        shapes = [((BLOCK, SIZE), F32), ((NT, BLOCK, SIZE), BF16)]
        outs = [flat, block_of((NT, BLOCK, SIZE))]
    return call(
        functools.partial(level_kernel, pair, len(tiles), len(back), len(earlier)),
        "level%d" % level,
        shapes,
        [SMEM] * 4 + [pick, pick, block_of((NT, BLOCK, SIZE))] + [ANY] * len(tiles) + [flat] * (len(back) + len(earlier)),
        outs,
        (place, here, there, live, rhs, dinv, known, *tiles, *back, *earlier),
        [pltpu.VMEM((PLACES, SLOTS * SIZE, SIZE), BF16), pltpu.SemaphoreType.DMA((PLACES,))],
        flops=2 * 24 * BLOCK * SIZE * SIZE,
        moved=24 * SIZE * SIZE * 2,
    )


def local(rhs, dinv, factor, cols, live):
    place = lax.axis_index(COL).astype(jnp.int32).reshape(1)
    tiles = factor.transpose(0, 2, 1, 3)
    move = lambda array, pairs: lax.ppermute(array, COL, pairs)
    over_row = lambda array: lax.all_to_all(array, "row", 0, 0, tiled=True)

    gather = lambda array, axes: lax.all_gather(array, axes, axis=0, tiled=False)
    live = live.transpose(1, 0)

    own = cols.transpose(2, 1, 0).reshape(SLOTS, -1)
    here = jnp.stack([own] + [move(own, TURN[d]) for d in range(1, CHIPS)])
    there = move(here, SWAP)
    cut0 = cut_call(tiles, 0)
    gathered0 = gather(cut0, COL)
    early, cut0 = lax.optimization_barrier((rhs, cut0))
    answer0, spread0, cut2, cut5 = first_call(place, early, dinv, tiles, (2, 5))
    gathered2, gathered5 = gather(cut2, COL), gather(cut5, COL)

    def send(picked):
        return [picked[0]] + [move(picked[d], TURN[d]) for d in range(1, CHIPS)]

    def give_back(sums):
        return [sums[0]] + [move(sums[d], TURN[CHIPS - d]) for d in range(1, CHIPS)]

    known0 = over_row(spread0)
    picked = pick_call("pick13", (1, 3), place, here, there, known0)
    later, known0, *picked = lax.optimization_barrier((tiles, known0, *picked))
    swapped = move(later, SWAP)
    got = send(picked)
    answer1, spread1 = level_call(1, 0, place, here, there, live, rhs, dinv, known0, [gathered0], [], [])
    spread1, *got = lax.optimization_barrier((spread1, *got))
    known1 = over_row(spread1)

    sums = partial_call("partial13", (1, 3), place, live, got, [], tiles, swapped)
    sums2, sums3 = sums[:CHIPS], sums[CHIPS:]
    back2 = give_back(sums2)
    known1, *back2 = lax.optimization_barrier((known1, *back2))
    picked = pick_call("pick4", (4,), place, here, there, known1)
    known1, *picked = lax.optimization_barrier((known1, *picked))
    got = send(picked)
    answer2, spread2 = level_call(2, 2, place, here, there, live, rhs, dinv, known1, [gathered2], back2, [])
    spread2, *got = lax.optimization_barrier((spread2, *got))
    known2 = over_row(spread2)

    sums3 = partial_call("partial4", (4,), place, live, got, sums3, tiles, swapped)
    (solved,) = level_call(
        3, 5, place, here, there, live, rhs, dinv, known2, [gathered5], give_back(sums3), [answer0, answer1, answer2]
    )
    return solved.transpose(0, 2, 1)


def solution(mesh):
    rows, places = mesh.devices.shape
    mesh = jax.sharding.Mesh(mesh.devices.reshape(rows, places // 2, 2), ("row",) + COL)
    in_specs = (
        P(None, "row", None),
        P(None, "row", None),
        P(None, "row", COL, None),
        P(None, "row", COL),
        P(None, "row"),
    )
    out_specs = P(None, "row", COL)
    return jax.shard_map(local, mesh=mesh, in_specs=in_specs, out_specs=out_specs, check_vma=False)
```
